128 devices in a mesh: section: 8 (over z, core), dp: 2 (over x_lo), tensor: 8 (over x_hi, y).
Axes of the slice: x: 4 (x_hi: 2, x_lo: 2; x = x_hi * 2 + x_lo), y: 4, z: 4, core: 2. Of those that a mesh axis runs over, the one named last changes fastest.
Arguments:
- patches: bfloat16 [16, 1024, 3200], P(('section', 'dp'), 'tensor'), may hold values from -4 to 4
- norm_gain: float32 [3200], replicated, may hold values from 0.1 to 1.9
- w_qkv: bfloat16 [3200, 3, 3072], P(None, None, 'tensor')
- q_gain: float32 [3072], P('tensor')
- k_gain: float32 [3072], P('tensor')
- w_out: bfloat16 [3072, 3200], P('tensor'), may hold values from -0.109375 to 0.109375
- layer_scale: float32 [3200], replicated, may hold values from 0.5 to 1.5
- w_proj: bfloat16 [12800, 4096], P(None, 'tensor'), may hold values from -0.0546875 to 0.0546875
- text_embed: bfloat16 [16, 768, 4096], P(('section', 'dp'), None, 'tensor'), may hold values from -6 to 6
- tile_counts: int32 [16], replicated, may hold values from 0 to 2, as said below
- image_offsets: int32 [16], replicated, may hold values from 0 to 256
- tile_slots: int32 [16], replicated, may hold values from 0 to 15, as said below
Outputs:
- llm_input: bfloat16 [16, 768, 4096], P(('section', 'dp'), None, 'tensor')
The draws below stay inside these ranges and needn't reach their ends.
Inputs may be any that keep to these rules, and one draw needn't show every extreme that they name: `tile_counts`: the counts sum to 16; the largest is exactly 2, and some sequence has no tile. `tile_slots`: a permutation of the packed positions.
All inputs are finite; a program needn't handle non-finite values.
Results may differ from the reference program's by a relative error of at most 0.012.
Values may be sent and summed in bfloat16 or wider, within the bound.
A program may use at most 128 MiB of HBM per device.

```python
import jax
import jax.numpy as jnp
from jax import lax

D = 3200
HEADS = 24
HD = 128
GRID = 32
TOK = 1024
ROWS_OUT = 256
WL = 4096
TEXT_LEN = 256
TILE_MEAN = 1
TILE_CAP = 2
GROUPS = 16
LIVE = 16
SEQ_LEN = 768


def draw_patches(key, part):
    key = jax.random.fold_in(key, 13)
    key_a = jax.random.fold_in(key, 0)
    base = jax.random.normal(key_a, (LIVE, TOK, D), jnp.float32)
    return jnp.clip(base, -4.0, 4.0).astype(jnp.bfloat16)


def head_ramp(top):
    steps = jnp.arange(HEADS, dtype=jnp.float32) / (HEADS - 1)
    return jnp.repeat(top ** steps, HD)


def draw_w_qkv(key, part):
    key = jax.random.fold_in(key, 11)
    key_a, key_b, key_c = jax.random.split(key, 3)
    width = HEADS * HD
    factor = D ** (-0.5)
    query_block = jax.random.normal(key_a, (D, width), jnp.float32) * factor
    value_block = jax.random.normal(key_c, (D, width), jnp.float32) * factor
    key_block = jax.random.normal(key_b, (D, width), jnp.float32) * factor
    ramp = head_ramp(3.16)
    query_block = query_block * ramp[None, :]
    key_block = key_block * ramp[None, :]
    return jnp.stack([query_block, key_block, value_block], axis=1).astype(jnp.bfloat16)


def draw_q_gain(key, part):
    key = jax.random.fold_in(key, 5)
    return jax.random.uniform(key, (HEADS * HD,), jnp.float32, 0.6, 1.4)


def draw_k_gain(key, part):
    key = jax.random.fold_in(key, 7)
    return jax.random.uniform(key, (HEADS * HD,), jnp.float32, 0.6, 1.4)


def draw_tile_counts(key, part):
    key = jax.random.fold_in(key, 17)
    key_a, key_b = jax.random.split(key)
    rest = jax.random.permutation(key_a, GROUPS - 1) + 1
    order = jnp.concatenate([jnp.zeros((1,), rest.dtype), rest])
    moved = jax.random.randint(key_b, (GROUPS // 2,), 0, TILE_MEAN + 1)
    moved = moved.at[0].set(TILE_MEAN)
    by_rank = jnp.stack([TILE_MEAN + moved, TILE_MEAN - moved], axis=1).reshape(GROUPS)
    counts = jnp.zeros((GROUPS,), jnp.int32).at[order].set(by_rank.astype(jnp.int32))
    return counts.astype(jnp.int32)


def draw_tile_slots(key, part):
    key = jax.random.fold_in(key, 19)
    rest = jax.random.permutation(key, LIVE - 1) + 1
    fixed = jnp.concatenate([jnp.zeros((1,), rest.dtype), rest])
    return ((fixed + LIVE // 2) % LIVE).astype(jnp.int32)


def with_ends(entries, rng, low, largest):
    longest = entries.shape.index(max(entries.shape))
    spots = []
    for shift in (0, 1):
        where = [jax.random.randint(jax.random.fold_in(rng, axis), (), 0, length) for axis, length in enumerate(entries.shape)]
        where[longest] = (where[longest] + shift) % entries.shape[longest]
        spots.append(tuple(where))
    return entries.at[spots[0]].set(low).at[spots[1]].set(largest)


def levels(stream_key, shape, pieces, least, high):
    def one(dim, shards_of):
        steps = jax.random.uniform(jax.random.fold_in(jax.random.fold_in(stream_key, 6), dim), (shards_of,), jnp.float32, least / len(pieces), high / len(pieces))
        return jnp.repeat(jnp.exp(steps), shape[dim] // shards_of).reshape((-1,) + (1,) * (len(shape) - dim - 1))

    loudness = one(*pieces[0])
    for cut in pieces[1:]:
        loudness = loudness * one(*cut)
    return loudness


def normal_values(key, dims, scale, limit, cuts=(), held_as=jnp.bfloat16):
    entries = scale * jax.random.normal(key, dims, jnp.float32)
    if cuts:
        entries = entries * levels(key, dims, cuts, -0.22, 0.18)
    return jnp.clip(entries, -limit, limit).astype(held_as)


def setup_inputs(seed: int = 0) -> dict:
    splits = jax.random.split(jax.random.key(seed), 13)
    return {
        "patches": draw_patches(jax.random.fold_in(splits[12], 71), 0),
        "norm_gain": jnp.clip(1.0 + 0.18 * jax.random.normal(splits[1], (D,), jnp.float32), 0.1, 1.9),
        "w_qkv": draw_w_qkv(jax.random.fold_in(splits[12], 71), 0),
        "q_gain": draw_q_gain(jax.random.fold_in(splits[12], 71), 0),
        "k_gain": draw_k_gain(jax.random.fold_in(splits[12], 71), 0),
        "w_out": normal_values(splits[5], (HEADS * HD, D), (HEADS * HD) ** -0.5, 0.109375, ((0, 8),)),
        "layer_scale": jnp.clip(jax.random.uniform(splits[6], (D,), jnp.float32, 0.5, 1.5), 0.5, 1.5),
        "w_proj": normal_values(splits[7], (4 * D, WL), (4 * D) ** -0.5, 0.0546875, ((1, 8),)),
        "text_embed": normal_values(splits[8], (GROUPS, SEQ_LEN, WL), 1.0, 6.0, ((0, 16), (2, 8))),
        "tile_counts": draw_tile_counts(jax.random.fold_in(splits[12], 71), 0),
        "image_offsets": with_ends(jax.random.randint(splits[10], (GROUPS,), 0, TEXT_LEN + 1), jax.random.fold_in(splits[10], 1), 0, TEXT_LEN).astype(jnp.int32),
        "tile_slots": draw_tile_slots(jax.random.fold_in(splits[12], 71), 0),
    }


def rms_scale(values, gain):
    mean_square = lax.optimization_barrier(jnp.mean(values * values, axis=-1, keepdims=True))
    return values * lax.rsqrt(mean_square + 1e-06) * gain

def encode_tile(tile, norm_gain, w_flat, q_gain, k_gain, w_out, layer_scale, w_proj):
    tile_f = tile.astype(jnp.float32)
    normed = rms_scale(tile_f, norm_gain.astype(jnp.float32)).astype(jnp.bfloat16)
    stacked = jnp.dot(normed, w_flat, preferred_element_type=jnp.float32)
    full_width = HEADS * HD
    queries = rms_scale(stacked[:, :full_width], q_gain.astype(jnp.float32)).astype(jnp.bfloat16)
    key_rows = rms_scale(stacked[:, full_width:2 * full_width], k_gain.astype(jnp.float32)).astype(jnp.bfloat16)
    value_rows = stacked[:, 2 * full_width:].astype(jnp.bfloat16)
    queries = queries.reshape(TOK, HEADS, HD).astype(jnp.float32)
    key_rows = key_rows.reshape(TOK, HEADS, HD).astype(jnp.float32)
    value_rows = value_rows.reshape(TOK, HEADS, HD).astype(jnp.float32)
    scores = jnp.einsum('qhd,khd->hqk', queries, key_rows) * HD ** (-0.5)
    weights = jax.nn.softmax(scores, axis=-1).astype(jnp.bfloat16)
    mixed = jnp.einsum('hqk,khd->qhd', weights.astype(jnp.float32), value_rows)
    mixed = mixed.astype(jnp.bfloat16).reshape(TOK, full_width)
    branch = jnp.dot(mixed, w_out, preferred_element_type=jnp.float32)
    encoded = (tile_f + layer_scale.astype(jnp.float32) * branch).astype(jnp.bfloat16)
    half_grid = GRID // 2
    merged = encoded.reshape(half_grid, 2, half_grid, 2, D).transpose(0, 2, 1, 3, 4).reshape(ROWS_OUT, 4 * D)
    return jnp.dot(merged, w_proj, preferred_element_type=jnp.float32).astype(jnp.bfloat16)

def reference(patches, norm_gain, w_qkv, q_gain, k_gain, w_out, layer_scale, w_proj, text_embed, tile_counts, image_offsets, tile_slots):
    w_flat = w_qkv.reshape(D, 3 * HEADS * HD)

    def one_tile(tile):
        return encode_tile(tile, norm_gain, w_flat, q_gain, k_gain, w_out, layer_scale, w_proj)
    projected = lax.map(one_tile, patches)
    counts = tile_counts.astype(jnp.int32)
    first_tile = (jnp.cumsum(counts) - counts).astype(jnp.int32)
    slot_table = tile_slots.astype(jnp.int32)

    def place(operands):
        text_rows, first, count, offset = operands
        slots = jnp.arange(TILE_CAP, dtype=jnp.int32)
        logical = jnp.minimum(first + slots, LIVE - 1).astype(jnp.int32)
        index_rows = jnp.take(slot_table, logical, axis=0).astype(jnp.int32)
        block = jnp.take(projected, index_rows, axis=0)
        block = jnp.where((slots < count)[:, None, None], block, jnp.zeros_like(block))
        block = block.reshape(TILE_CAP * ROWS_OUT, WL)
        placed = lax.dynamic_update_slice(jnp.zeros((SEQ_LEN, WL), projected.dtype), block, (offset.astype(jnp.int32), jnp.int32(0)))
        positions = jnp.arange(SEQ_LEN, dtype=jnp.int32)
        inside = (positions >= offset) & (positions < offset + count * ROWS_OUT)
        return jnp.where(inside[:, None], placed, text_rows)
    return lax.map(place, (text_embed, first_tile, counts, image_offsets.astype(jnp.int32)))
```

```python
import functools

import jax
import jax.numpy as jnp
from jax import lax
from jax.experimental import pallas as pl
from jax.experimental.pallas import tpu as pltpu
from jax.sharding import PartitionSpec as P

D = 3200
HEADS = 24
HD = 128
CH = 128
LH = 3
LW = 384
F32 = jnp.float32
BF16 = jnp.bfloat16
MESH = pl.DeviceIdType.MESH
EPS = 1e-06
VMEM = pltpu.VMEM
PARAMS = dict(has_side_effects=True, vmem_limit_bytes=60 * 1024 * 1024)

O0, X0, O1, OM, X1, XM, O2, X2 = range(8)

GATHER = (
    (O0, 0, 64, "x", X0),
    (O0, 0, 64, "p", OM),
    (O0, 0, 64, "m", O1),
    (O0, 64, 64, "p", OM),
    (O0, 64, 64, "m", O1),
    (O0, 64, 64, "x", X0),
    (OM, 0, 32, "p", O2),
    (O1, 32, 32, "m", O2),
    (X0, 0, 64, "p", XM),
    (X0, 0, 64, "m", X1),
    (XM, 0, 32, "p", X2),
    (X1, 32, 32, "m", X2),
    (OM, 64, 32, "p", O2),
    (O1, 96, 32, "m", O2),
    (OM, 64, 64, "x", XM),
    (O1, 64, 64, "x", X1),
    (O2, 64, 32, "x", X2),
    (O2, 96, 32, "x", X2),
)

SCATTER = (
    (X2, 0, 32, "p", X1, 0),
    (X2, 32, 32, "m", XM, 32),
    (X2, 64, 64, "x", O2, 64),
    (O2, 0, 32, "p", O1, 128),
    (O2, 32, 32, "m", OM, 160),
    (X1, 64, 64, "x", O1, 192),
    (XM, 64, 64, "x", OM, 256),
    (X1, 0, 64, "p", X0, 320),
    (XM, 0, 64, "m", X0, 384),
    (O1, 0, 64, "p", O0, 448),
    (OM, 0, 64, "m", O0, 512),
    (O2, 64, 32, "p", O1, 576),
    (O2, 96, 32, "m", OM, 608),
    (X0, 64, 64, "x", O0, 640),
    (X0, 0, 64, "x", O0, 704),
    (O1, 64, 64, "p", O0, 768),
    (OM, 64, 64, "m", O0, 832),
)
LAND_ROWS = 896


def where_am_i():
    t = lax.axis_index("tensor")
    xh = t // 4
    y = lax.rem(t, 4)
    return t, xh, y


def directions():
    _, xh, y = where_am_i()
    return {
        "p": {"tensor": xh * 4 + lax.rem(y + 1, 4)},
        "m": {"tensor": xh * 4 + lax.rem(y + 3, 4)},
        "x": {"tensor": (1 - xh) * 4 + y},
    }


def slot_chunks():
    _, xh, y = where_am_i()
    near, far = xh * 4, (1 - xh) * 4
    up, down, opposite = lax.rem(y + 1, 4), lax.rem(y + 3, 4), lax.rem(y + 2, 4)
    return (near + y, far + y, near + up, near + down, far + up, far + down, near + opposite, far + opposite)


def gather_copies(buf, send, recv):
    where = directions()
    return [
        pltpu.make_async_remote_copy(
            src_ref=buf.at[src, pl.ds(row, rows)],
            dst_ref=buf.at[dst, pl.ds(row, rows)],
            send_sem=send.at[i],
            recv_sem=recv.at[i],
            device_id=where[way],
            device_id_type=MESH,
        )
        for i, (src, row, rows, way, dst) in enumerate(GATHER)
    ]


def scatter_copies(buf, land, send, recv):
    where = directions()
    return [
        pltpu.make_async_remote_copy(
            src_ref=buf.at[src, pl.ds(row, rows)],
            dst_ref=land.at[pl.ds(place, rows)],
            send_sem=send.at[i],
            recv_sem=recv.at[i],
            device_id=where[way],
            device_id_type=MESH,
        )
        for i, (src, row, rows, way, dst, place) in enumerate(SCATTER)
    ]


def merge_order(row0, rows):
    r = lax.broadcasted_iota(jnp.int32, (rows, CH), 0) + row0
    c = lax.broadcasted_iota(jnp.int32, (rows, CH), 1)
    a, b, i, j = r // 64, (r // 32) % 2, (r // 16) % 2, r % 16
    return ((2 * i + a) * 32 + 2 * j + b == c).astype(F32).astype(BF16)


def qkv_kernel(patches, gain, w_hbm, q_gain, k_gain, q_out, k_out, v_out, xg, w, qk, sums, w_sem, send, recv, s_send, s_recv):
    t, _, _ = where_am_i()
    chunk_of = slot_chunks()
    w_copies = [pltpu.make_async_copy(w_hbm.at[j], w.at[j], w_sem.at[j]) for j in range(3)]
    for c in w_copies:
        c.start()
    barrier = pltpu.get_barrier_semaphore()
    for k in range(1, 8):
        pl.semaphore_signal(barrier, inc=1, device_id={"tensor": lax.rem(t + k, 8)}, device_id_type=MESH)

    def norm(row0):
        x = jnp.dot(merge_order(row0, 32), patches[...], preferred_element_type=F32)
        scale = lax.rsqrt(jnp.mean(x * x, axis=-1, keepdims=True) + EPS)
        xg[O0, pl.ds(row0, 32)] = (x * scale * gain[...]).astype(BF16)

    cp = gather_copies(xg, send, recv)
    norm(0)
    norm(32)
    pl.semaphore_wait(barrier, 7)
    for i in (0, 1, 2):
        cp[i].start()
    norm(64)
    norm(96)
    for i in (3, 4, 5):
        cp[i].start()
    for c in w_copies:
        c.wait()

    def after(done, *then):
        cp[done].wait_recv()
        for i in then:
            cp[i].start()

    def project(g):
        x = xg[2 * g : 2 * g + 2].reshape(2 * CH, D)
        rows = pl.ds(2 * g * CH, 2 * CH)
        for j in range(2):
            part = jnp.dot(x, w[j], preferred_element_type=F32)
            qk[j, rows] = part
            for u in range(2):
                p = part[u * CH : (u + 1) * CH]
                sq = p * p
                sq = sq[:, :HD] + sq[:, HD : 2 * HD] + sq[:, 2 * HD :]
                row = jnp.sum(jnp.transpose(sq), axis=0, keepdims=True)
                sums[t, chunk_of[2 * g + u], :, j * HD : (j + 1) * HD] = row
        part = jnp.dot(x, w[2], preferred_element_type=F32).astype(BF16)
        for h in range(LH):
            v_out[h, rows] = part[:, h * HD : (h + 1) * HD]

    after(1, 6)
    after(2, 7)
    after(0, 8, 9)
    after(3, 12, 14)
    after(4, 13, 15)
    after(5)
    project(0)
    after(8, 10)
    after(9, 11)
    after(12, 16)
    after(13, 17)
    project(1)
    after(14)
    after(15)
    project(2)
    for i in (6, 7, 10, 11, 16, 17):
        after(i)
    project(3)

    s_copies = [
        pltpu.make_async_remote_copy(
            src_ref=sums.at[t],
            dst_ref=sums.at[t],
            send_sem=s_send.at[k],
            recv_sem=s_recv.at[k],
            device_id={"tensor": lax.rem(t + k, 8)},
            device_id_type=MESH,
        )
        for k in range(1, 8)
    ]
    for c in s_copies:
        c.start()
    for c in cp:
        c.wait_send()
    for k in range(1, 8):
        pltpu.make_async_remote_copy(
            src_ref=sums.at[lax.rem(t + 8 - k, 8)],
            dst_ref=sums.at[lax.rem(t + 8 - k, 8)],
            send_sem=s_send.at[k],
            recv_sem=s_recv.at[k],
            device_id={"tensor": lax.rem(t + k, 8)},
            device_id_type=MESH,
        ).wait_recv()
    for slot in range(8):
        total = sums[0, chunk_of[slot]]
        for other in range(1, 8):
            total = total + sums[other, chunk_of[slot]]
        scale = lax.rsqrt(total / (HEADS * HD) + EPS)
        rows = pl.ds(slot * CH, CH)
        for j, (out, g, extra) in enumerate(((q_out, q_gain, HD**-0.5), (k_out, k_gain, 1.0))):
            col = jnp.transpose(jnp.broadcast_to(scale[:, j * HD : (j + 1) * HD], (CH, HD))) * extra
            for h in range(LH):
                lanes = slice(h * HD, (h + 1) * HD)
                out[h, rows] = (qk[j, rows, lanes] * col * g[:, lanes]).astype(BF16)
    for c in s_copies:
        c.wait_send()


def encode_kernel(
    q, k, v, patches, layer_scale, wo_hbm, wp_hbm, counts, slots, feats,
    wo, wp, ob, land, xg, mixed, proj, pieces, picked, arrive,
    w_sem, r_send, r_recv, send, recv, a_send, a_recv, b_send, b_recv,
):
    chunk_of = slot_chunks()
    section = lax.axis_index("section")
    dp = lax.axis_index("dp")
    me = section * 2 + dp
    wo_copy = pltpu.make_async_copy(wo_hbm, wo, w_sem.at[0])
    wp_copy = pltpu.make_async_copy(wp_hbm, wp, w_sem.at[1])
    wo_copy.start()
    wp_copy.start()
    barrier = pltpu.get_barrier_semaphore()
    where = directions()
    for way in ("p", "m", "x"):
        pl.semaphore_signal(barrier, inc=1, device_id=where[way], device_id_type=MESH)

    def group(index):
        return {"section": index // 2, "dp": lax.rem(index, 2)}

    for n in range(1, 16):
        pl.semaphore_signal(barrier, inc=1, device_id=group(lax.rem(me + n, 16)), device_id_type=MESH)
    rc = scatter_copies(ob, land, r_send, r_recv)
    gc = gather_copies(xg, send, recv)

    def attend(first):
        def one(step, _):
            h = step % LH
            r0 = pl.multiple_of((step // LH) * CH, CH)
            rows = pl.ds(first * CH + r0, CH)
            scores = lax.dot_general(q[h, rows], k[h], (((1,), (1,)), ((), ())), preferred_element_type=F32)
            e = jnp.exp(scores - jnp.max(scores, axis=-1, keepdims=True))
            total = jnp.sum(e, axis=-1, keepdims=True)
            part = jnp.dot(e.astype(BF16), v[h], preferred_element_type=F32)
            mixed[h, pl.ds(r0, CH)] = (part / total).astype(BF16)
            return _

        lax.fori_loop(0, 2 * LH, one, 0)

        both = jnp.concatenate([mixed[h] for h in range(LH)], axis=1)
        for n0 in range(0, D, 640):
            part = jnp.dot(both, wo[:, n0 : n0 + 640], preferred_element_type=F32).astype(BF16)
            ob[first, :, n0 : n0 + 640] = part[:CH]
            ob[first + 1, :, n0 : n0 + 640] = part[CH:]

    def add(i):
        rc[i].wait_recv()
        _, row, rows, _, dst, place = SCATTER[i]
        for r in range(0, rows, 32):
            total = ob[dst, row + r : row + r + 32].astype(F32) + land[place + r : place + r + 32].astype(F32)
            ob[dst, row + r : row + r + 32] = total.astype(BF16)

    wo_copy.wait()
    attend(O2)
    pl.semaphore_wait(barrier, 18)
    for i in (0, 1, 2, 3, 4):
        rc[i].start()
    attend(X1)
    for i in (5, 6):
        rc[i].start()
    add(0)
    rc[7].start()
    add(1)
    rc[8].start()
    attend(O1)
    add(3)
    rc[9].start()
    add(4)
    rc[10].start()
    add(2)
    rc[11].start()
    rc[12].start()
    attend(O0)
    rc[13].start()
    add(7)
    add(8)
    rc[14].start()
    add(5)
    add(11)
    rc[15].start()
    add(6)
    add(12)
    rc[16].start()
    add(9)
    add(10)
    add(13)

    def encode(row0):
        base = jnp.dot(merge_order(row0, 32), patches[...], preferred_element_type=F32)
        branch = ob[O0, row0 : row0 + 32].astype(F32)
        xg[O0, pl.ds(row0, 32)] = (base + layer_scale[...] * branch).astype(BF16)

    add(14)
    encode(0)
    encode(32)
    for i in (0, 1, 2):
        gc[i].start()
    add(15)
    add(16)
    encode(64)
    encode(96)
    for i in (3, 4, 5):
        gc[i].start()
    for c in rc:
        c.wait_send()

    def after(done, *then):
        gc[done].wait_recv()
        for i in then:
            gc[i].start()

    def project(ab):
        x = xg[:, ab * 32 : (ab + 1) * 32, :].reshape(8 * 32, D)
        return jnp.dot(x, wp[ab * D : (ab + 1) * D, :], preferred_element_type=F32)

    after(1, 6)
    after(2, 7)
    after(0, 8, 9)
    after(3, 12, 14)
    after(4, 13, 15)
    after(5)
    after(8, 10)
    after(9, 11)
    after(12, 16)
    after(13, 17)
    wp_copy.wait()
    for i in (6, 7, 10, 11):
        after(i)
    total = project(0) + project(1)
    for i in (14, 15, 16, 17):
        after(i)
    total = (total + project(2) + project(3)).astype(BF16)
    for slot in range(8):
        proj[pl.ds(2 * chunk_of[slot], 2)] = total[slot * 32 : (slot + 1) * 32].reshape(2, 16, 512)
    for c in gc:
        c.wait_send()

    first = [
        pltpu.make_async_remote_copy(
            src_ref=proj.at[lax.rem(me + n, 16)],
            dst_ref=pieces.at[me],
            send_sem=a_send.at[n],
            recv_sem=a_recv.at[n],
            device_id=group(lax.rem(me + n, 16)),
            device_id_type=MESH,
        )
        for n in range(1, 16)
    ]
    for c in first:
        c.start()
    pieces[me] = proj[me]
    for n in range(1, 16):
        source = lax.rem(me + 16 - n, 16)
        pltpu.make_async_remote_copy(
            src_ref=pieces.at[source],
            dst_ref=pieces.at[source],
            send_sem=a_send.at[n],
            recv_sem=a_recv.at[n],
            device_id=group(lax.rem(me + n, 16)),
            device_id_type=MESH,
        ).wait_recv()
    start = jnp.int32(0)
    for g in range(16):
        for s in range(2):
            tile = slots[jnp.minimum(start + s, 15)]
            picked[g, s] = pieces[tile]
        start = start + counts[g]
    second = [
        pltpu.make_async_remote_copy(
            src_ref=picked.at[lax.rem(me + n, 16)],
            dst_ref=arrive.at[me],
            send_sem=b_send.at[n],
            recv_sem=b_recv.at[n],
            device_id=group(lax.rem(me + n, 16)),
            device_id_type=MESH,
        )
        for n in range(1, 16)
    ]
    for c in second:
        c.start()
    arrive[me] = picked[me]
    for n in range(1, 16):
        source = lax.rem(me + 16 - n, 16)
        pltpu.make_async_remote_copy(
            src_ref=arrive.at[source],
            dst_ref=arrive.at[source],
            send_sem=b_send.at[n],
            recv_sem=b_recv.at[n],
            device_id=group(lax.rem(me + n, 16)),
            device_id_type=MESH,
        ).wait_recv()
    for n in range(16):
        for s in range(2):
            feats[s * 256 + n * 16 : s * 256 + n * 16 + 16, :] = arrive[n, s]
    for c in first:
        c.wait_send()
    for c in second:
        c.wait_send()


def place_kernel(feats, text, counts, offsets, out):
    me = lax.axis_index("section") * 2 + lax.axis_index("dp")
    rows = counts[me] * 256
    offset = offsets[me]
    seq = text.shape[0]
    for r0 in range(0, seq, 256):
        r = lax.broadcasted_iota(jnp.int32, (256, 512), 0) + r0 - offset
        c = lax.broadcasted_iota(jnp.int32, (256, 512), 1)
        pick = (r == c).astype(F32).astype(BF16)
        moved = jnp.dot(pick, feats[...], preferred_element_type=F32)
        inside = (r >= 0) & (r < rows)
        out[r0 : r0 + 256, :] = jnp.where(inside, moved, text[r0 : r0 + 256, :].astype(F32)).astype(BF16)


def spec(space):
    return pl.BlockSpec(memory_space=space)


def shards(
    patches,
    norm_gain,
    w_qkv,
    q_gain,
    k_gain,
    w_out,
    layer_scale,
    w_proj,
    text_embed,
    tile_counts,
    image_offsets,
    tile_slots,
):
    chunk = patches[0]
    heads = jax.ShapeDtypeStruct((LH, 8 * CH, HD), BF16)
    dma = pltpu.SemaphoreType.DMA
    q, k, v = pl.pallas_call(
        qkv_kernel,
        out_shape=(heads, heads, heads),
        in_specs=[spec(VMEM), spec(VMEM), spec(pl.ANY), spec(VMEM), spec(VMEM)],
        out_specs=(spec(VMEM), spec(VMEM), spec(VMEM)),
        scratch_shapes=[
            VMEM((8, CH, D), BF16),
            VMEM((3, D, LW), BF16),
            VMEM((2, 8 * CH, LW), F32),
            VMEM((8, 8, 1, 2 * HD), F32),
            dma((3,)),
            dma((18,)),
            dma((18,)),
            dma((8,)),
            dma((8,)),
        ],
        compiler_params=pltpu.CompilerParams(collective_id=0, **PARAMS),
        name="qkv",
    )(chunk, norm_gain.reshape(1, D), w_qkv.transpose(1, 0, 2), q_gain.reshape(1, LW), k_gain.reshape(1, LW))
    smem = pltpu.SMEM
    feats = pl.pallas_call(
        encode_kernel,
        out_shape=jax.ShapeDtypeStruct((512, 512), BF16),
        in_specs=[spec(VMEM)] * 5 + [spec(pl.ANY)] * 2 + [spec(smem)] * 2,
        out_specs=spec(VMEM),
        scratch_shapes=[
            VMEM((LW, D), BF16),
            VMEM((4 * D, 512), BF16),
            VMEM((8, CH, D), BF16),
            VMEM((LAND_ROWS, D), BF16),
            VMEM((8, CH, D), BF16),
            VMEM((LH, 2 * CH, HD), BF16),
            VMEM((16, 16, 512), BF16),
            VMEM((16, 16, 512), BF16),
            VMEM((16, 2, 16, 512), BF16),
            VMEM((16, 2, 16, 512), BF16),
            dma((2,)),
            dma((17,)),
            dma((17,)),
            dma((18,)),
            dma((18,)),
            dma((16,)),
            dma((16,)),
            dma((16,)),
            dma((16,)),
        ],
        compiler_params=pltpu.CompilerParams(collective_id=1, **PARAMS),
        name="encode",
    )(q, k, v, chunk, layer_scale.reshape(1, D), w_out, w_proj, tile_counts, tile_slots)
    out = pl.pallas_call(
        place_kernel,
        out_shape=jax.ShapeDtypeStruct(text_embed.shape[1:], BF16),
        in_specs=[spec(VMEM)] * 2 + [spec(smem)] * 2,
        out_specs=spec(VMEM),
        compiler_params=pltpu.CompilerParams(vmem_limit_bytes=32 * 1024 * 1024),
        name="place",
    )(feats, text_embed[0], tile_counts, image_offsets)
    return out[None]


def solution(mesh):
    placed = (
        P(("section", "dp"), "tensor", None),
        P(),
        P(None, None, "tensor"),
        P("tensor"),
        P("tensor"),
        P("tensor", None),
        P(),
        P(None, "tensor"),
        P(("section", "dp"), None, "tensor"),
        P(),
        P(),
        P(),
    )
    return jax.shard_map(
        shards,
        mesh=mesh,
        in_specs=placed,
        out_specs=P(("section", "dp"), None, "tensor"),
        check_vma=False,
    )
```

```python
import jax
import jax.numpy as jnp
from jax import lax
from jax.experimental import pallas as pl
from jax.experimental.pallas import tpu as pltpu
from jax.sharding import PartitionSpec as P

D = 3200
HEADS = 24
HD = 128
CH = 128
LH = 3
LW = 384
F32 = jnp.float32
BF16 = jnp.bfloat16
MESH = pl.DeviceIdType.MESH
EPS = 1e-06
VMEM = pltpu.VMEM
PARAMS = dict(has_side_effects=True, vmem_limit_bytes=62 * 1024 * 1024)

O0, X0, O1, OM, X1, XM, O2, X2 = range(8)
N2, N1, NM, N0 = range(4)

GATHER = (
    (O0, 0, 80, "x", X0),
    (O0, 0, 80, "p", OM),
    (O0, 0, 80, "m", O1),
    (O0, 80, 48, "p", OM),
    (O0, 80, 48, "m", O1),
    (O0, 80, 48, "x", X0),
    (OM, 0, 48, "p", O2),
    (O1, 48, 32, "m", O2),
    (X0, 0, 80, "p", XM),
    (X0, 0, 80, "m", X1),
    (XM, 0, 48, "p", X2),
    (X1, 48, 32, "m", X2),
    (OM, 80, 16, "p", O2),
    (O1, 96, 32, "m", O2),
    (OM, 80, 48, "x", XM),
    (O1, 80, 48, "x", X1),
    (O2, 80, 16, "x", X2),
    (O2, 96, 32, "x", X2),
)

SCATTER = tuple(
    copy
    for b in (0, 64)
    for copy in (
        (N2, b, "p", N1),
        (N2, b + 32, "m", NM),
        (N1, b + 32, "p", N0),
        (N1, b, "p", N0),
        (NM, b, "m", N0),
        (NM, b + 32, "m", N0),
    )
)

SPREAD = tuple(
    copy
    for b in (0, 64)
    for copy in ((N0, b, 64, "p", NM), (N0, b, 64, "m", N1), (NM, b, 32, "p", N2), (N1, b + 32, 32, "m", N2))
)

SETS = ((48, 32), (400, 208), (400, 208), (400, 208), (400, 208))
WEIGHTS = ((0, 0, "u"), (0, 0, "d"), (0, 0, "c"), (-2, 1, "u"), (-2, 0, "c"), (2, 2, "d"), (2, 0, "c"), (4, 1, "c"), (4, 2, "c"))


def where_am_i():
    t = lax.axis_index("tensor")
    return t, t // 4, lax.rem(t, 4)


def directions():
    _, xh, y = where_am_i()
    section = lax.axis_index("section")
    return {
        "p": {"tensor": xh * 4 + lax.rem(y + 1, 4)},
        "m": {"tensor": xh * 4 + lax.rem(y + 3, 4)},
        "x": {"tensor": (1 - xh) * 4 + y},
        "cross": {"dp": 1 - lax.axis_index("dp"), "tensor": (1 - xh) * 4 + y},
        "u": {"section": lax.rem(section + 2, 8)},
        "d": {"section": lax.rem(section + 6, 8)},
        "c": {"section": section + 1 - 2 * lax.rem(section, 2)},
    }


def slot_chunks():
    _, xh, y = where_am_i()
    near, far = xh * 4, (1 - xh) * 4
    up, down, opposite = lax.rem(y + 1, 4), lax.rem(y + 3, 4), lax.rem(y + 2, 4)
    return (near + y, far + y, near + up, near + down, far + up, far + down, near + opposite, far + opposite)


def remote(src, dst, send, recv, target):
    return pltpu.make_async_remote_copy(
        src_ref=src, dst_ref=dst, send_sem=send, recv_sem=recv, device_id=target, device_id_type=MESH
    )


def table_copies(table, buf, send, recv):
    where = directions()
    return [
        remote(buf.at[src, pl.ds(row, rows)], buf.at[dst, pl.ds(row, rows)], send.at[i], recv.at[i], where[way])
        for i, (src, row, rows, way, dst) in enumerate(table)
    ]


def weight_copies(number, source, buf, base, send, recv):
    rows, first = SETS[number]
    section = lax.axis_index("section")
    where = directions()

    def part(ref, offset, which):
        start = base + lax.rem(section + 8 + offset, 8) * rows
        start, count = ((start, rows), (start, first), (start + first, rows - first))[which]
        return ref.at[pl.ds(pl.multiple_of(start, 16), count)]

    copies = [remote(part(source, 0, 0), part(buf, 0, 0), send.at[number, 0], recv.at[number, 0], where["cross"])]
    for i, (offset, which, way) in enumerate(WEIGHTS):
        there = part(buf, offset, which)
        copies.append(remote(there, there, send.at[number, i + 1], recv.at[number, i + 1], where[way]))
    return copies


def merge_order(row0, rows):
    r = lax.broadcasted_iota(jnp.int32, (rows, CH), 0) + row0
    c = lax.broadcasted_iota(jnp.int32, (rows, CH), 1)
    a, b, i, j = r // 64, (r // 32) % 2, (r // 16) % 2, r % 16
    return ((2 * i + a) * 32 + 2 * j + b == c).astype(F32).astype(BF16)


def encode_kernel(
    patches, gain, w_hbm, q_gain, k_gain, layer_scale, wo_hbm, wp_hbm, counts, slots, feats,
    xg, w, qk, sums, q, k, v, wo, wp, mix, far, ob, proj, pieces, picked, arrive,
    w_sem, g_send, g_recv, s_send, s_recv, x_send, x_recv, m_send, m_recv, r_send, r_recv, e_send, e_recv,
    a_send, a_recv, b_send, b_recv,
):
    t, xh, y = where_am_i()
    opp = (1 - xh) * 4 + y
    chunk_of = slot_chunks()
    me = lax.axis_index("section") * 2 + lax.axis_index("dp")

    def group(index, tensor):
        return {"section": index // 2, "dp": lax.rem(index, 2), "tensor": tensor}

    w_copies = [pltpu.make_async_copy(w_hbm.at[j], w.at[j], w_sem.at[j]) for j in range(3)]
    own_copies = [
        pltpu.make_async_copy(wo_hbm, wo.at[0], w_sem.at[3]),
        pltpu.make_async_copy(wp_hbm, wp.at[0], w_sem.at[4]),
    ]
    for c in w_copies + own_copies:
        c.start()
    barrier = pltpu.get_barrier_semaphore()
    for n in range(1, 8):
        pl.semaphore_signal(barrier, inc=1, device_id={"tensor": lax.rem(t + n, 8)}, device_id_type=MESH)
    for n in range(1, 16):
        for tensor in (t, opp):
            target = group(lax.rem(me + n, 16), tensor)
            pl.semaphore_signal(barrier, inc=1, device_id=target, device_id_type=MESH)

    def norm(row0, rows):
        x = jnp.dot(merge_order(row0, rows), patches[...], preferred_element_type=F32)
        scale = lax.rsqrt(jnp.mean(x * x, axis=-1, keepdims=True) + EPS)
        xg[O0, pl.ds(row0, rows)] = (x * scale * gain[...].reshape(1, D)).astype(BF16)

    gc = table_copies(GATHER, xg, g_send, g_recv)
    wc = [weight_copies(0, wo_hbm, wo.at[1], 0, x_send, x_recv)]
    wc += [weight_copies(1 + ab, wp_hbm, wp.at[1], ab * D, x_send, x_recv) for ab in range(4)]

    def weights_cross(n):
        wc[n][0].start()

    def weights_turn(n):
        wc[n][0].wait_recv()
        for i in (1, 2, 3):
            wc[n][i].start()

    def weights_forward(n):
        wc[n][1].wait_recv()
        wc[n][4].start()
        wc[n][5].start()
        wc[n][2].wait_recv()
        wc[n][6].start()
        wc[n][7].start()

    def weights_last(n):
        wc[n][4].wait_recv()
        wc[n][8].start()
        wc[n][6].wait_recv()
        wc[n][9].start()

    def weights_here(n):
        for i in (3, 5, 7, 8, 9):
            wc[n][i].wait_recv()

    norm(0, 32)
    norm(32, 32)
    norm(64, 16)
    pl.semaphore_wait(barrier, 37)
    for i in (0, 1, 2):
        gc[i].start()
    weights_cross(0)
    norm(80, 16)
    norm(96, 32)
    for i in (3, 4, 5):
        gc[i].start()
    for c in w_copies:
        c.wait()

    def after(done, *then):
        gc[done].wait_recv()
        for i in then:
            gc[i].start()

    def project_qkv(g):
        x = xg[2 * g : 2 * g + 2].reshape(2 * CH, D)
        rows = pl.ds(2 * g * CH, 2 * CH)
        for j in range(2):
            part = jnp.dot(x, w[j], preferred_element_type=F32)
            qk[j, rows] = part
            for u in range(2):
                p = part[u * CH : (u + 1) * CH]
                sq = p * p
                sq = sq[:, :HD] + sq[:, HD : 2 * HD] + sq[:, 2 * HD :]
                row = jnp.sum(jnp.transpose(sq), axis=0, keepdims=True)
                sums[t, chunk_of[2 * g + u], :, j * HD : (j + 1) * HD] = row
        part = jnp.dot(x, w[2], preferred_element_type=F32).astype(BF16)
        for h in range(LH):
            v[h, rows] = part[:, h * HD : (h + 1) * HD]

    after(1, 6)
    after(2, 7)
    after(0, 8, 9)
    after(3, 12, 14)
    after(4, 13, 15)
    after(5)
    project_qkv(0)
    after(8, 10)
    after(9, 11)
    after(12, 16)
    after(13, 17)
    weights_turn(0)
    weights_cross(1)
    project_qkv(1)
    weights_forward(0)
    after(14)
    after(15)
    project_qkv(2)
    weights_last(0)
    weights_cross(2)
    for i in (6, 7, 10, 11, 16, 17):
        after(i)
    project_qkv(3)

    s_copies = [
        remote(sums.at[t], sums.at[t], s_send.at[n], s_recv.at[n], {"tensor": lax.rem(t + n, 8)}) for n in range(1, 8)
    ]
    for c in gc:
        c.wait_send()
    for c in s_copies:
        c.start()
    weights_turn(1)
    for n in range(1, 8):
        there = sums.at[lax.rem(t + 8 - n, 8)]
        remote(there, there, s_send.at[n], s_recv.at[n], {"tensor": lax.rem(t + n, 8)}).wait_recv()
    for slot in range(8):
        total = sums[0, chunk_of[slot]]
        for other in range(1, 8):
            total = total + sums[other, chunk_of[slot]]
        scale = lax.rsqrt(total / (HEADS * HD) + EPS)
        rows = pl.ds(slot * CH, CH)
        for j, (out, g, extra) in enumerate(((q, q_gain, HD**-0.5), (k, k_gain, 1.0))):
            col = jnp.transpose(jnp.broadcast_to(scale[:, j * HD : (j + 1) * HD], (CH, HD))) * extra
            gains = g[...].reshape(1, LW)
            for h in range(LH):
                lanes = slice(h * HD, (h + 1) * HD)
                out[h, rows] = (qk[j, rows, lanes] * col * gains[:, lanes]).astype(BF16)

    def attend(first, second, dst, place):
        def one(h, _):
            for n, slot in enumerate((first, second)):
                rows = pl.ds(slot * CH, CH)
                scores = lax.dot_general(q[h, rows], k[h], (((1,), (1,)), ((), ())), preferred_element_type=F32)
                e = jnp.exp(scores - jnp.max(scores, axis=-1, keepdims=True))
                total = jnp.sum(e, axis=-1, keepdims=True)
                part = jnp.dot(e.astype(BF16), v[h], preferred_element_type=F32)
                dst[place + n, :, pl.ds(pl.multiple_of(h * HD, HD), HD)] = (part / total).astype(BF16)
            return _

        lax.fori_loop(0, LH, one, 0)

    mc = [remote(far.at[n], mix.at[1, n], m_send.at[n], m_recv.at[n], directions()["x"]) for n in range(4)]
    rc = [
        remote(ob.at[src, pl.ds(row, 32)], xg.at[4 + i // 4, pl.ds(32 * (i % 4), 32)], r_send.at[i], r_recv.at[i], directions()[way])
        for i, (src, row, way, _) in enumerate(SCATTER)
    ]
    ec = table_copies(SPREAD, xg, e_send, e_recv)

    def branch(n):
        for i in (n, n + 1):
            mc[i].wait_recv()
        mine = mix[0, n : n + 2].reshape(2 * CH, LW)
        other = mix[1, n : n + 2].reshape(2 * CH, LW)
        for n0 in range(0, D, 640):
            cols = slice(n0, n0 + 640)
            part = jnp.dot(mine, wo[0, :, cols], preferred_element_type=F32)
            part = (part + jnp.dot(other, wo[1, :, cols], preferred_element_type=F32)).astype(BF16)
            ob[n, :, cols] = part[:CH]
            ob[n + 1, :, cols] = part[CH:]

    def add(i):
        rc[i].wait_recv()
        _, row, _, dst = SCATTER[i]
        total = ob[dst, row : row + 32].astype(F32) + xg[4 + i // 4, 32 * (i % 4) : 32 * (i % 4) + 32].astype(F32)
        ob[dst, row : row + 32] = total.astype(BF16)

    attend(X2, X1, far, 0)
    mc[0].start()
    mc[1].start()
    weights_cross(3)
    attend(O2, O1, mix.at[0], 0)
    own_copies[0].wait()
    weights_here(0)
    branch(0)
    for i in (0, 1, 6, 7, 2, 8):
        rc[i].start()
    weights_turn(2)
    weights_forward(1)
    attend(XM, X0, far, 2)
    mc[2].start()
    mc[3].start()
    weights_cross(4)
    attend(OM, O0, mix.at[0], 2)
    branch(2)
    for i in (4, 10):
        rc[i].start()
    for b in (0, 6):
        add(b)
        rc[b + 3].start()
        add(b + 1)
        rc[b + 5].start()
    weights_last(1)
    weights_turn(3)
    weights_forward(2)

    def encode(row0):
        base = jnp.dot(merge_order(row0, 32), patches[...], preferred_element_type=F32)
        total = ob[N0, row0 : row0 + 32].astype(F32)
        xg[N0, pl.ds(row0, 32)] = (base + layer_scale[...].reshape(1, D) * total).astype(BF16)

    def encode_half(half):
        for i in (2, 4, 3, 5):
            add(6 * half + i)
        encode(64 * half)
        encode(64 * half + 32)
        ec[4 * half].start()
        ec[4 * half + 1].start()

    encode_half(0)
    weights_last(2)
    weights_turn(4)
    weights_forward(3)
    encode_half(1)
    for c in rc + mc:
        c.wait_send()

    def forward(half):
        ec[4 * half].wait_recv()
        ec[4 * half + 2].start()
        ec[4 * half + 1].wait_recv()
        ec[4 * half + 3].start()

    def project(ab, total):
        weights_here(1 + ab)
        x = xg[0:4, ab * 32 : (ab + 1) * 32, :].reshape(4 * 32, D)
        rows = slice(ab * D, (ab + 1) * D)
        return [sofar + jnp.dot(x, wp[c, rows, :], preferred_element_type=F32) for c, sofar in enumerate(total)]

    forward(0)
    weights_last(3)
    weights_forward(4)
    forward(1)
    own_copies[1].wait()
    ec[2].wait_recv()
    ec[3].wait_recv()
    total = project(0, [jnp.zeros((CH, 512), F32)] * 2)
    weights_last(4)
    total = project(1, total)
    ec[6].wait_recv()
    ec[7].wait_recv()
    total = project(2, total)
    total = project(3, total)
    for c in range(2):
        out = total[c].astype(BF16)
        for n, slot in ((N2, O2), (N1, O1), (NM, OM), (N0, O0)):
            place = 2 * lax.rem(chunk_of[slot], 4)
            proj[c, pl.ds(place, 2)] = out[n * 32 : (n + 1) * 32].reshape(2, 16, 512)
    for c in ec + [c for copies in wc for c in copies]:
        c.wait_send()

    mine = me // 8 == xh

    def piece_copy(n, c):
        m = lax.rem(me + n, 8)
        target = group(8 * xh + m, (t, opp)[c])
        return remote(proj.at[c, m], pieces.at[me], a_send.at[c, n], a_recv.at[me], target)

    def first_copies(act):
        for n in range(1, 8):
            for c in range(2):
                act(piece_copy(n, c))
        act(piece_copy(0, 1))

        @pl.when(jnp.logical_not(mine))
        def _():
            act(piece_copy(0, 0))

    first_copies(lambda c: c.start())

    @pl.when(mine)
    def _():
        pieces[me] = proj[0, lax.rem(me, 8)]

    def piece_here(g):
        remote(pieces.at[g], pieces.at[g], a_send.at[0, 0], a_recv.at[g], group(me, opp)).wait_recv()

    for n in range(1, 16):
        piece_here(lax.rem(me + n, 16))

    @pl.when(jnp.logical_not(mine))
    def _():
        piece_here(me)

    start = jnp.int32(0)
    for g in range(16):
        for s in range(2):
            tile = slots[jnp.minimum(start + s, 15)]
            picked[g, s] = pieces[tile]
        start = start + counts[g]
    second = [
        remote(
            picked.at[lax.rem(me + n, 16)], arrive.at[me], b_send.at[n], b_recv.at[n], group(lax.rem(me + n, 16), t)
        )
        for n in range(1, 16)
    ]
    for c in second:
        c.start()
    arrive[me] = picked[me]
    for n in range(1, 16):
        there = arrive.at[lax.rem(me + 16 - n, 16)]
        remote(there, there, b_send.at[n], b_recv.at[n], group(lax.rem(me + n, 16), t)).wait_recv()
    for n in range(16):
        for s in range(2):
            feats[s * 256 + n * 16 : s * 256 + n * 16 + 16, :] = arrive[n, s]
    first_copies(lambda c: c.wait_send())
    for c in s_copies + second:
        c.wait_send()


def place_kernel(feats, text, counts, offsets, out):
    me = lax.axis_index("section") * 2 + lax.axis_index("dp")
    rows = counts[me] * 256
    offset = offsets[me]
    seq = text.shape[0]
    for r0 in range(0, seq, 256):
        r = lax.broadcasted_iota(jnp.int32, (256, 512), 0) + r0 - offset
        c = lax.broadcasted_iota(jnp.int32, (256, 512), 1)
        pick = (r == c).astype(F32).astype(BF16)
        moved = jnp.dot(pick, feats[...], preferred_element_type=F32)
        inside = (r >= 0) & (r < rows)
        out[r0 : r0 + 256, :] = jnp.where(inside, moved, text[r0 : r0 + 256, :].astype(F32)).astype(BF16)


def spec(space):
    return pl.BlockSpec(memory_space=space)


def shards(
    patches,
    norm_gain,
    w_qkv,
    q_gain,
    k_gain,
    w_out,
    layer_scale,
    w_proj,
    text_embed,
    tile_counts,
    image_offsets,
    tile_slots,
):
    dma = pltpu.SemaphoreType.DMA
    smem = pltpu.SMEM
    heads = VMEM((LH, 8 * CH, HD), BF16)
    feats = pl.pallas_call(
        encode_kernel,
        out_shape=jax.ShapeDtypeStruct((512, 512), BF16),
        in_specs=[spec(s) for s in (VMEM, VMEM, pl.ANY, VMEM, VMEM, VMEM, pl.ANY, pl.ANY, smem, smem)],
        out_specs=spec(VMEM),
        scratch_shapes=[
            VMEM((8, CH, D), BF16),
            VMEM((3, D, LW), BF16),
            VMEM((2, 8 * CH, LW), F32),
            VMEM((8, 8, 1, 2 * HD), F32),
            heads,
            heads,
            heads,
            VMEM((2, LW, D), BF16),
            VMEM((2, 4 * D, 512), BF16),
            VMEM((2, 4, CH, LW), BF16),
            VMEM((4, CH, LW), BF16),
            VMEM((4, CH, D), BF16),
            VMEM((2, 8, 16, 512), BF16),
            VMEM((16, 16, 512), BF16),
            VMEM((16, 2, 16, 512), BF16),
            VMEM((16, 2, 16, 512), BF16),
            dma((5,)),
            dma((len(GATHER),)),
            dma((len(GATHER),)),
            dma((8,)),
            dma((8,)),
            dma((len(SETS), 10)),
            dma((len(SETS), 10)),
            dma((4,)),
            dma((4,)),
            dma((len(SCATTER),)),
            dma((len(SCATTER),)),
            dma((len(SPREAD),)),
            dma((len(SPREAD),)),
            dma((2, 8)),
            dma((16,)),
            dma((16,)),
            dma((16,)),
        ],
        compiler_params=pltpu.CompilerParams(collective_id=0, **PARAMS),
        name="encode",
    )(
        patches[0],
        norm_gain,
        w_qkv.transpose(1, 0, 2),
        q_gain,
        k_gain,
        layer_scale,
        w_out,
        w_proj,
        tile_counts,
        tile_slots,
    )
    out = pl.pallas_call(
        place_kernel,
        out_shape=jax.ShapeDtypeStruct(text_embed.shape[1:], BF16),
        in_specs=[spec(VMEM)] * 2 + [spec(smem)] * 2,
        out_specs=spec(VMEM),
        compiler_params=pltpu.CompilerParams(vmem_limit_bytes=32 * 1024 * 1024),
        name="place",
    )(feats, text_embed[0], tile_counts, image_offsets)
    return out[None]


def solution(mesh):
    placed = (
        P(("section", "dp"), "tensor", None),
        P(),
        P(None, None, "tensor"),
        P("tensor"),
        P("tensor"),
        P("tensor", None),
        P(),
        P(None, "tensor"),
        P(("section", "dp"), None, "tensor"),
        P(),
        P(),
        P(),
    )
    return jax.shard_map(
        shards,
        mesh=mesh,
        in_specs=placed,
        out_specs=P(("section", "dp"), None, "tensor"),
        check_vma=False,
    )
```

```python
import jax
import jax.numpy as jnp
from jax import lax
from jax.experimental import pallas as pl
from jax.experimental.pallas import tpu as pltpu
from jax.sharding import PartitionSpec as P

D = 3200
HEADS = 24
HD = 128
CH = 128
LH = 3
LW = 384
F32 = jnp.float32
BF16 = jnp.bfloat16
MESH = pl.DeviceIdType.MESH
EPS = 1e-06
LOG2E = 1.4426950408889634
VMEM = pltpu.VMEM
PARAMS = dict(has_side_effects=True, vmem_limit_bytes=62 * 1024 * 1024)

O0, X0, O1, OM, X1, XM, O2, X2 = range(8)
N2, N1, NM, N0 = range(4)

GATHER = (
    (O0, 0, 96, "x", X0),
    (O0, 0, 96, "p", OM),
    (O0, 0, 96, "m", O1),
    (O0, 96, 32, "p", OM),
    (O0, 96, 32, "m", O1),
    (O0, 96, 32, "x", X0),
    (OM, 0, 48, "p", O2),
    (O1, 48, 48, "m", O2),
    (X0, 0, 96, "p", XM),
    (X0, 0, 96, "m", X1),
    (XM, 0, 48, "p", X2),
    (X1, 48, 48, "m", X2),
    (OM, 96, 16, "p", O2),
    (O1, 112, 16, "m", O2),
    (OM, 96, 32, "x", XM),
    (O1, 96, 32, "x", X1),
    (O2, 96, 16, "x", X2),
    (O2, 112, 16, "x", X2),
)

SCATTER = tuple(
    copy
    for b in (0, 64)
    for copy in (
        (N2, b, "p", N1),
        (N2, b + 32, "m", NM),
        (N1, b + 32, "p", N0),
        (N1, b, "p", N0),
        (NM, b, "m", N0),
        (NM, b + 32, "m", N0),
    )
)

SPREAD = tuple(
    copy
    for b in (0, 64)
    for copy in ((N0, b, 64, "p", NM), (N0, b, 64, "m", N1), (NM, b, 32, "p", N2), (N1, b + 32, 32, "m", N2))
)

SETS = ((48, 32), (400, 208), (400, 208), (400, 208), (400, 208))
WEIGHTS = ((0, 0, "u"), (0, 0, "d"), (0, 0, "c"), (-2, 1, "u"), (-2, 0, "c"), (2, 2, "d"), (2, 0, "c"), (4, 1, "c"), (4, 2, "c"))


def where_am_i():
    t = lax.axis_index("tensor")
    return t, t // 4, lax.rem(t, 4)


def directions():
    _, xh, y = where_am_i()
    section = lax.axis_index("section")
    return {
        "p": {"tensor": xh * 4 + lax.rem(y + 1, 4)},
        "m": {"tensor": xh * 4 + lax.rem(y + 3, 4)},
        "x": {"tensor": (1 - xh) * 4 + y},
        "cross": {"dp": 1 - lax.axis_index("dp"), "tensor": (1 - xh) * 4 + y},
        "u": {"section": lax.rem(section + 2, 8)},
        "d": {"section": lax.rem(section + 6, 8)},
        "c": {"section": section + 1 - 2 * lax.rem(section, 2)},
    }


def slot_chunks():
    _, xh, y = where_am_i()
    near, far = xh * 4, (1 - xh) * 4
    up, down, opposite = lax.rem(y + 1, 4), lax.rem(y + 3, 4), lax.rem(y + 2, 4)
    return (near + y, far + y, near + up, near + down, far + up, far + down, near + opposite, far + opposite)


def remote(src, dst, send, recv, target):
    return pltpu.make_async_remote_copy(
        src_ref=src, dst_ref=dst, send_sem=send, recv_sem=recv, device_id=target, device_id_type=MESH
    )


def table_copies(table, buf, send, recv):
    where = directions()
    return [
        remote(buf.at[src, pl.ds(row, rows)], buf.at[dst, pl.ds(row, rows)], send.at[i], recv.at[i], where[way])
        for i, (src, row, rows, way, dst) in enumerate(table)
    ]


def weight_copies(number, source, buf, base, send, recv, source_base=0):
    rows, first = SETS[number]
    section = lax.axis_index("section")
    where = directions()

    def part(ref, offset, which, base=base):
        start = base + lax.rem(section + 8 + offset, 8) * rows
        start, count = ((start, rows), (start, first), (start + first, rows - first))[which]
        return ref.at[pl.ds(pl.multiple_of(start, 16), count)]

    copies = [remote(part(source, 0, 0, source_base), part(buf, 0, 0), send.at[number, 0], recv.at[number, 0], where["cross"])]
    for i, (offset, which, way) in enumerate(WEIGHTS):
        there = part(buf, offset, which)
        copies.append(remote(there, there, send.at[number, i + 1], recv.at[number, i + 1], where[way]))
    return copies


def merge_order(row0, rows):
    r = lax.broadcasted_iota(jnp.int32, (rows, CH), 0) + row0
    c = lax.broadcasted_iota(jnp.int32, (rows, CH), 1)
    a, b, i, j = r // 64, (r // 32) % 2, (r // 16) % 2, r % 16
    return ((2 * i + a) * 32 + 2 * j + b == c).astype(F32).astype(BF16)


def encode_kernel(
    patches, gain, w_hbm, q_gain, k_gain, layer_scale, wo_hbm, wp_hbm, counts, slots, feats,
    xg, w, qk, sums, q, k, v, wo, wp, mix, far, ob, proj, pieces, picked, arrive,
    w_sem, g_send, g_recv, s_send, s_recv, x_send, x_recv, m_send, m_recv, r_send, r_recv, e_send, e_recv,
    a_send, a_recv, b_send, b_recv,
):
    t, xh, y = where_am_i()
    opp = (1 - xh) * 4 + y
    chunk_of = slot_chunks()
    me = lax.axis_index("section") * 2 + lax.axis_index("dp")

    def group(index, tensor):
        return {"section": index // 2, "dp": lax.rem(index, 2), "tensor": tensor}

    w_copies = [pltpu.make_async_copy(w_hbm.at[j], w.at[j], w_sem.at[j]) for j in range(3)]
    own_copies = [
        pltpu.make_async_copy(wo_hbm, wo.at[pl.ds(0, LW)], w_sem.at[3]),
        pltpu.make_async_copy(wp_hbm, wp.at[0], w_sem.at[4]),
    ]
    for c in w_copies + own_copies:
        c.start()
    barrier = pltpu.get_barrier_semaphore()
    for n in range(1, 8):
        pl.semaphore_signal(barrier, inc=1, device_id={"tensor": lax.rem(t + n, 8)}, device_id_type=MESH)
    for way in ("cross", "u", "d", "c"):
        pl.semaphore_signal(barrier, inc=1, device_id=directions()[way], device_id_type=MESH)

    def norm(row0, rows):
        x = jnp.dot(merge_order(row0, rows), patches[...], preferred_element_type=F32)
        scale = lax.rsqrt(jnp.mean(x * x, axis=-1, keepdims=True) + EPS)
        xg[O0, pl.ds(row0, rows)] = (x * scale * gain[...].reshape(1, D)).astype(BF16)

    gc = table_copies(GATHER, xg, g_send, g_recv)
    wc = [weight_copies(0, wo_hbm, wo, LW, x_send, x_recv)]
    wc += [weight_copies(1 + ab, wp_hbm, wp.at[1], ab * D, x_send, x_recv, ab * D) for ab in range(4)]

    def weights_cross(n):
        wc[n][0].start()

    def weights_turn(n):
        wc[n][0].wait_recv()
        for i in (1, 2, 3):
            wc[n][i].start()

    def weights_forward(n):
        wc[n][1].wait_recv()
        wc[n][4].start()
        wc[n][5].start()
        wc[n][2].wait_recv()
        wc[n][6].start()
        wc[n][7].start()

    def weights_last(n):
        wc[n][4].wait_recv()
        wc[n][8].start()
        wc[n][6].wait_recv()
        wc[n][9].start()

    def weights_here(n):
        for i in (3, 5, 7, 8, 9):
            wc[n][i].wait_recv()

    norm(0, 32)
    norm(32, 32)
    norm(64, 32)
    pl.semaphore_wait(barrier, 11)
    for i in (0, 1, 2):
        gc[i].start()
    weights_cross(0)
    norm(96, 32)
    for i in (3, 4, 5):
        gc[i].start()
    for c in w_copies:
        c.wait()

    def after(done, *then):
        gc[done].wait_recv()
        for i in then:
            gc[i].start()

    def project_qk(g):
        x = xg[2 * g : 2 * g + 2].reshape(2 * CH, D)
        rows = pl.ds(2 * g * CH, 2 * CH)
        for j in range(2):
            part = jnp.dot(x, w[j], preferred_element_type=F32)
            qk[j, rows] = part
            for u in range(2):
                p = part[u * CH : (u + 1) * CH]
                sq = p * p
                sq = sq[:, :HD] + sq[:, HD : 2 * HD] + sq[:, 2 * HD :]
                row = jnp.sum(jnp.transpose(sq), axis=0, keepdims=True)
                sums[t, chunk_of[2 * g + u], :, j * HD : (j + 1) * HD] = row

    def project_v(g):
        x = xg[2 * g : 2 * g + 2].reshape(2 * CH, D)
        part = jnp.dot(x, w[2], preferred_element_type=F32).astype(BF16)
        for h in range(LH):
            v[h, pl.ds(2 * g * CH, 2 * CH), :HD] = part[:, h * HD : (h + 1) * HD]

    after(1, 6)
    after(2, 7)
    after(0, 8, 9)
    after(3, 12, 14)
    after(4, 13, 15)
    after(5)
    project_qk(0)
    project_v(0)
    after(8, 10)
    after(9, 11)
    after(12, 16)
    after(13, 17)
    weights_turn(0)
    weights_cross(1)
    project_qk(1)
    project_v(1)
    v[:, :, HD:] = jnp.ones((LH, 8 * CH, HD), BF16)
    weights_forward(0)
    after(14)
    after(15)
    project_qk(2)
    project_v(2)
    weights_last(0)
    for i in (6, 7, 16, 17, 10, 11):
        after(i)
    weights_cross(2)
    project_qk(3)

    s_copies = [
        remote(sums.at[t], sums.at[t], s_send.at[n], s_recv.at[n], {"tensor": lax.rem(t + n, 8)}) for n in range(1, 8)
    ]
    for c in gc:
        c.wait_send()
    for c in s_copies:
        c.start()
    project_v(3)
    weights_turn(1)
    for n in range(1, 8):
        there = sums.at[lax.rem(t + 8 - n, 8)]
        remote(there, there, s_send.at[n], s_recv.at[n], {"tensor": lax.rem(t + n, 8)}).wait_recv()
    for slot in range(8):
        total = sums[0, chunk_of[slot]]
        for other in range(1, 8):
            total = total + sums[other, chunk_of[slot]]
        scale = lax.rsqrt(total / (HEADS * HD) + EPS)
        rows = pl.ds(slot * CH, CH)
        for j, (out, g, extra) in enumerate(((q, q_gain, HD**-0.5 * LOG2E), (k, k_gain, 1.0))):
            col = jnp.transpose(jnp.broadcast_to(scale[:, j * HD : (j + 1) * HD], (CH, HD))) * extra
            gains = g[...].reshape(1, LW)
            for h in range(LH):
                lanes = slice(h * HD, (h + 1) * HD)
                out[h, rows] = (qk[j, rows, lanes] * col * gains[:, lanes]).astype(BF16)

    def attend(slot, *places):
        def one(h, _):
            rows = pl.ds(slot * CH, 2 * CH)
            scores = lax.dot_general(q[h, rows], k[h], (((1,), (1,)), ((), ())), preferred_element_type=F32)
            e = jnp.exp2(scores - jnp.max(scores, axis=-1, keepdims=True)).astype(BF16)
            part = jnp.dot(e, v[h], preferred_element_type=F32)
            part = (part[:, :HD] / part[:, HD:]).astype(BF16)
            lanes = pl.ds(pl.multiple_of(h * HD, HD), HD)
            for n, (dst, place) in enumerate(places):
                dst[place, :, lanes] = part[n * CH : (n + 1) * CH]
            return _

        lax.fori_loop(0, LH, one, 0)

    mc = [remote(far.at[n], mix.at[1, n], m_send.at[n], m_recv.at[n], directions()["x"]) for n in range(4)]
    rc = [
        remote(ob.at[src, pl.ds(row, 32)], xg.at[4 + i // 4, pl.ds(32 * (i % 4), 32)], r_send.at[i], r_recv.at[i], directions()[way])
        for i, (src, row, way, _) in enumerate(SCATTER)
    ]
    ec = table_copies(SPREAD, xg, e_send, e_recv)

    def branch(n, count):
        for i in range(n, n + count):
            mc[i].wait_recv()
        x = jnp.concatenate([mix[c, n : n + count].reshape(count * CH, LW) for c in range(2)], axis=1)
        for n0 in range(0, D, 1280):
            cols = slice(n0, min(n0 + 1280, D))
            part = jnp.dot(x, wo[:, cols], preferred_element_type=F32).astype(BF16)
            for i in range(count):
                ob[n + i, :, cols] = part[i * CH : (i + 1) * CH]

    def add(i):
        rc[i].wait_recv()
        _, row, _, dst = SCATTER[i]
        total = ob[dst, row : row + 32].astype(F32) + xg[4 + i // 4, 32 * (i % 4) : 32 * (i % 4) + 32].astype(F32)
        ob[dst, row : row + 32] = total.astype(BF16)

    own, off = mix.at[0], far
    attend(O2, (own, N2), (off, N2))
    mc[N2].start()
    attend(X1, (off, N1), (off, NM))
    mc[N1].start()
    mc[NM].start()
    own_copies[0].wait()
    weights_here(0)
    branch(N2, 1)
    for i in (0, 1, 6, 7):
        rc[i].start()
    attend(O1, (own, N1), (own, NM))
    branch(N1, 2)
    for i in (2, 4):
        rc[i].start()
    weights_turn(2)
    weights_cross(3)
    attend(O0, (own, N0), (off, N0))
    mc[N0].start()
    add(0)
    rc[3].start()
    add(1)
    rc[5].start()
    for i in (8, 10):
        rc[i].start()
    weights_forward(1)
    branch(N0, 1)
    weights_cross(4)
    add(6)
    rc[9].start()
    add(7)
    rc[11].start()
    weights_turn(3)

    def encode(row0):
        base = jnp.dot(merge_order(row0, 32), patches[...], preferred_element_type=F32)
        total = ob[N0, row0 : row0 + 32].astype(F32)
        xg[N0, pl.ds(row0, 32)] = (base + layer_scale[...].reshape(1, D) * total).astype(BF16)

    def encode_half(half):
        for i in (2, 4, 3, 5):
            add(6 * half + i)
        encode(64 * half)
        encode(64 * half + 32)
        ec[4 * half].start()
        ec[4 * half + 1].start()

    encode_half(0)
    weights_last(1)
    weights_forward(2)
    weights_turn(4)
    encode_half(1)
    weights_forward(3)
    weights_last(2)
    for c in rc + mc:
        c.wait_send()

    def forward(half):
        ec[4 * half].wait_recv()
        ec[4 * half + 2].start()
        ec[4 * half + 1].wait_recv()
        ec[4 * half + 3].start()

    def project(ab, total):
        weights_here(1 + ab)
        x = xg[0:4, ab * 32 : (ab + 1) * 32, :].reshape(4 * 32, D)
        rows = slice(ab * D, (ab + 1) * D)
        return [sofar + jnp.dot(x, wp[c, rows, :], preferred_element_type=F32) for c, sofar in enumerate(total)]

    forward(0)
    weights_forward(4)
    weights_last(3)
    forward(1)
    own_copies[1].wait()
    ec[2].wait_recv()
    ec[3].wait_recv()
    total = project(0, [jnp.zeros((CH, 512), F32)] * 2)
    total = project(1, total)
    weights_last(4)
    ec[6].wait_recv()
    ec[7].wait_recv()
    total = project(2, total)
    total = project(3, total)
    for c in range(2):
        out = total[c].astype(BF16)
        for n, slot in ((N2, O2), (N1, O1), (NM, OM), (N0, O0)):
            place = 2 * lax.rem(chunk_of[slot], 4)
            proj[c, pl.ds(place, 2)] = out[n * 32 : (n + 1) * 32].reshape(2, 16, 512)
    for c in ec + [c for copies in wc for c in copies]:
        c.wait_send()

    mine = me // 8 == xh

    def piece_copy(n, c):
        m = lax.rem(me + n, 8)
        target = group(8 * xh + m, (t, opp)[c])
        return remote(proj.at[c, m], pieces.at[me], a_send.at[c, n], a_recv.at[me], target)

    def first_copies(act):
        for n in range(1, 8):
            for c in range(2):
                act(piece_copy(n, c))
        act(piece_copy(0, 1))

        @pl.when(jnp.logical_not(mine))
        def _():
            act(piece_copy(0, 0))

    first_copies(lambda c: c.start())

    @pl.when(mine)
    def _():
        pieces[me] = proj[0, lax.rem(me, 8)]

    def piece_here(g):
        remote(pieces.at[g], pieces.at[g], a_send.at[0, 0], a_recv.at[g], group(me, opp)).wait_recv()

    for n in range(1, 16):
        piece_here(lax.rem(me + n, 16))

    @pl.when(jnp.logical_not(mine))
    def _():
        piece_here(me)

    start = jnp.int32(0)
    for g in range(16):
        for s in range(2):
            tile = slots[jnp.minimum(start + s, 15)]
            picked[g, s] = pieces[tile]
        start = start + counts[g]
    second = [
        remote(
            picked.at[lax.rem(me + n, 16)], arrive.at[me], b_send.at[n], b_recv.at[n], group(lax.rem(me + n, 16), t)
        )
        for n in range(1, 16)
    ]
    for c in second:
        c.start()
    arrive[me] = picked[me]
    for n in range(1, 16):
        there = arrive.at[lax.rem(me + 16 - n, 16)]
        remote(there, there, b_send.at[n], b_recv.at[n], group(lax.rem(me + n, 16), t)).wait_recv()
    for n in range(16):
        for s in range(2):
            feats[s * 256 + n * 16 : s * 256 + n * 16 + 16, :] = arrive[n, s]
    first_copies(lambda c: c.wait_send())
    for c in s_copies + second:
        c.wait_send()


def place_kernel(feats, text, counts, offsets, out):
    me = lax.axis_index("section") * 2 + lax.axis_index("dp")
    rows = counts[me] * 256
    offset = offsets[me]
    seq = text.shape[0]
    for r0 in range(0, seq, 256):
        r = lax.broadcasted_iota(jnp.int32, (256, 512), 0) + r0 - offset
        c = lax.broadcasted_iota(jnp.int32, (256, 512), 1)
        pick = (r == c).astype(F32).astype(BF16)
        moved = jnp.dot(pick, feats[...], preferred_element_type=F32)
        inside = (r >= 0) & (r < rows)
        out[r0 : r0 + 256, :] = jnp.where(inside, moved, text[r0 : r0 + 256, :].astype(F32)).astype(BF16)


def spec(space):
    return pl.BlockSpec(memory_space=space)


def shards(
    patches,
    norm_gain,
    w_qkv,
    q_gain,
    k_gain,
    w_out,
    layer_scale,
    w_proj,
    text_embed,
    tile_counts,
    image_offsets,
    tile_slots,
):
    dma = pltpu.SemaphoreType.DMA
    smem = pltpu.SMEM
    heads = VMEM((LH, 8 * CH, HD), BF16)
    values = VMEM((LH, 8 * CH, 2 * HD), BF16)
    feats = pl.pallas_call(
        encode_kernel,
        out_shape=jax.ShapeDtypeStruct((512, 512), BF16),
        in_specs=[spec(s) for s in (VMEM, VMEM, pl.ANY, VMEM, VMEM, VMEM, pl.ANY, pl.ANY, smem, smem)],
        out_specs=spec(VMEM),
        scratch_shapes=[
            VMEM((8, CH, D), BF16),
            VMEM((3, D, LW), BF16),
            VMEM((2, 8 * CH, LW), F32),
            VMEM((8, 8, 1, 2 * HD), F32),
            heads,
            heads,
            values,
            VMEM((2 * LW, D), BF16),
            VMEM((2, 4 * D, 512), BF16),
            VMEM((2, 4, CH, LW), BF16),
            VMEM((4, CH, LW), BF16),
            VMEM((4, CH, D), BF16),
            VMEM((2, 8, 16, 512), BF16),
            VMEM((16, 16, 512), BF16),
            VMEM((16, 2, 16, 512), BF16),
            VMEM((16, 2, 16, 512), BF16),
            dma((5,)),
            dma((len(GATHER),)),
            dma((len(GATHER),)),
            dma((8,)),
            dma((8,)),
            dma((len(SETS), 10)),
            dma((len(SETS), 10)),
            dma((4,)),
            dma((4,)),
            dma((len(SCATTER),)),
            dma((len(SCATTER),)),
            dma((len(SPREAD),)),
            dma((len(SPREAD),)),
            dma((2, 8)),
            dma((16,)),
            dma((16,)),
            dma((16,)),
        ],
        compiler_params=pltpu.CompilerParams(collective_id=0, **PARAMS),
        name="encode",
    )(
        patches[0],
        norm_gain,
        w_qkv.transpose(1, 0, 2),
        q_gain,
        k_gain,
        layer_scale,
        w_out,
        w_proj,
        tile_counts,
        tile_slots,
    )
    out = pl.pallas_call(
        place_kernel,
        out_shape=jax.ShapeDtypeStruct(text_embed.shape[1:], BF16),
        in_specs=[spec(VMEM)] * 2 + [spec(smem)] * 2,
        out_specs=spec(VMEM),
        compiler_params=pltpu.CompilerParams(vmem_limit_bytes=32 * 1024 * 1024),
        name="place",
    )(feats, text_embed[0], tile_counts, image_offsets)
    return out[None]


def solution(mesh):
    placed = (
        P(("section", "dp"), "tensor", None),
        P(),
        P(None, None, "tensor"),
        P("tensor"),
        P("tensor"),
        P("tensor", None),
        P(),
        P(None, "tensor"),
        P(("section", "dp"), None, "tensor"),
        P(),
        P(),
        P(),
    )
    return jax.shard_map(
        shards,
        mesh=mesh,
        in_specs=placed,
        out_specs=P(("section", "dp"), None, "tensor"),
        check_vma=False,
    )
```

```python
import jax
import jax.numpy as jnp
from jax import lax
from jax.experimental import pallas as pl
from jax.experimental.pallas import tpu as pltpu
from jax.sharding import PartitionSpec as P

D = 3200
HEADS = 24
HD = 128
CH = 128
LH = 3
LW = 384
F32 = jnp.float32
BF16 = jnp.bfloat16
MESH = pl.DeviceIdType.MESH
EPS = 1e-06
LOG2E = 1.4426950408889634
VMEM = pltpu.VMEM
PARAMS = dict(has_side_effects=True, vmem_limit_bytes=62 * 1024 * 1024)

O0, X0, O1, OM, X1, XM, O2, X2 = range(8)
N2, N1, NM, N0 = range(4)

GATHER = (
    (O0, 0, 96, "x", X0),
    (O0, 0, 96, "p", OM),
    (O0, 0, 96, "m", O1),
    (O0, 96, 32, "p", OM),
    (O0, 96, 32, "m", O1),
    (O0, 96, 32, "x", X0),
    (OM, 0, 48, "p", O2),
    (O1, 48, 48, "m", O2),
    (X0, 0, 96, "p", XM),
    (X0, 0, 96, "m", X1),
    (XM, 0, 48, "p", X2),
    (X1, 48, 48, "m", X2),
    (OM, 96, 16, "p", O2),
    (O1, 112, 16, "m", O2),
    (OM, 96, 32, "x", XM),
    (O1, 96, 32, "x", X1),
    (O2, 96, 16, "x", X2),
    (O2, 112, 16, "x", X2),
)

SCATTER = tuple(
    copy
    for b in (0, 64)
    for copy in (
        (N2, b, "p", N1),
        (N2, b + 32, "m", NM),
        (N1, b + 32, "p", N0),
        (N1, b, "p", N0),
        (NM, b, "m", N0),
        (NM, b + 32, "m", N0),
    )
)

SPREAD = tuple(
    copy
    for b in (0, 64)
    for copy in ((N0, b, 64, "p", NM), (N0, b, 64, "m", N1), (NM, b, 32, "p", N2), (N1, b + 32, 32, "m", N2))
)

SETS = ((48, 32), (400, 208), (400, 208), (400, 208), (400, 208))
WEIGHTS = ((0, 0, "u"), (0, 0, "d"), (0, 0, "c"), (-2, 1, "u"), (-2, 0, "c"), (2, 2, "d"), (2, 0, "c"), (4, 1, "c"), (4, 2, "c"))


def where_am_i():
    t = lax.axis_index("tensor")
    return t, t // 4, lax.rem(t, 4)


def directions():
    _, xh, y = where_am_i()
    section = lax.axis_index("section")
    return {
        "p": {"tensor": xh * 4 + lax.rem(y + 1, 4)},
        "m": {"tensor": xh * 4 + lax.rem(y + 3, 4)},
        "x": {"tensor": (1 - xh) * 4 + y},
        "cross": {"dp": 1 - lax.axis_index("dp"), "tensor": (1 - xh) * 4 + y},
        "u": {"section": lax.rem(section + 2, 8)},
        "d": {"section": lax.rem(section + 6, 8)},
        "c": {"section": section + 1 - 2 * lax.rem(section, 2)},
    }


def slot_chunks():
    _, xh, y = where_am_i()
    near, far = xh * 4, (1 - xh) * 4
    up, down, opposite = lax.rem(y + 1, 4), lax.rem(y + 3, 4), lax.rem(y + 2, 4)
    return (near + y, far + y, near + up, near + down, far + up, far + down, near + opposite, far + opposite)


def remote(src, dst, send, recv, target):
    return pltpu.make_async_remote_copy(
        src_ref=src, dst_ref=dst, send_sem=send, recv_sem=recv, device_id=target, device_id_type=MESH
    )


def table_copies(table, buf, send, recv):
    where = directions()
    return [
        remote(buf.at[src, pl.ds(row, rows)], buf.at[dst, pl.ds(row, rows)], send.at[i], recv.at[i], where[way])
        for i, (src, row, rows, way, dst) in enumerate(table)
    ]


def weight_copies(number, source, buf, base, send, recv, source_base=0):
    rows, first = SETS[number]
    section = lax.axis_index("section")
    where = directions()

    def part(ref, offset, which, base=base):
        start = base + lax.rem(section + 8 + offset, 8) * rows
        start, count = ((start, rows), (start, first), (start + first, rows - first))[which]
        return ref.at[pl.ds(pl.multiple_of(start, 16), count)]

    copies = [remote(part(source, 0, 0, source_base), part(buf, 0, 0), send.at[number, 0], recv.at[number, 0], where["cross"])]
    for i, (offset, which, way) in enumerate(WEIGHTS):
        there = part(buf, offset, which)
        copies.append(remote(there, there, send.at[number, i + 1], recv.at[number, i + 1], where[way]))
    return copies


def merge_order(row0, rows):
    r = lax.broadcasted_iota(jnp.int32, (rows, CH), 0) + row0
    c = lax.broadcasted_iota(jnp.int32, (rows, CH), 1)
    a, b, i, j = r // 64, (r // 32) % 2, (r // 16) % 2, r % 16
    return ((2 * i + a) * 32 + 2 * j + b == c).astype(F32).astype(BF16)


def encode_kernel(
    patches, gain, w_hbm, q_gain, k_gain, layer_scale, wo_hbm, wp_hbm, counts, slots, feats,
    xg, w, qk, sums, q, k, v, wo, wp, mix, far, ob, proj, pieces, picked, arrive,
    w_sem, g_send, g_recv, s_send, s_recv, x_send, x_recv, m_send, m_recv, r_send, r_recv, e_send, e_recv,
    a_send, a_recv, b_send, b_recv,
):
    t, xh, y = where_am_i()
    opp = (1 - xh) * 4 + y
    chunk_of = slot_chunks()
    me = lax.axis_index("section") * 2 + lax.axis_index("dp")

    def group(index, tensor):
        return {"section": index // 2, "dp": lax.rem(index, 2), "tensor": tensor}

    w_copies = [pltpu.make_async_copy(w_hbm.at[j], w.at[j], w_sem.at[j]) for j in range(3)]
    own_copies = [
        pltpu.make_async_copy(wo_hbm, wo.at[pl.ds(0, LW)], w_sem.at[3]),
        pltpu.make_async_copy(wp_hbm, wp.at[0], w_sem.at[4]),
    ]
    for c in w_copies + own_copies:
        c.start()
    barrier = pltpu.get_barrier_semaphore()
    for n in range(1, 8):
        pl.semaphore_signal(barrier, inc=1, device_id={"tensor": lax.rem(t + n, 8)}, device_id_type=MESH)
    for way in ("cross", "u", "d", "c"):
        pl.semaphore_signal(barrier, inc=1, device_id=directions()[way], device_id_type=MESH)

    def norm(row0, rows):
        x = jnp.dot(merge_order(row0, rows), patches[...], preferred_element_type=F32)
        scale = lax.rsqrt(jnp.mean(x * x, axis=-1, keepdims=True) + EPS)
        xg[O0, pl.ds(row0, rows)] = (x * scale * gain[...].reshape(1, D)).astype(BF16)

    gc = table_copies(GATHER, xg, g_send, g_recv)
    wc = [weight_copies(0, wo_hbm, wo, LW, x_send, x_recv)]
    wc += [weight_copies(1 + ab, wp_hbm, wp.at[1], ab * D, x_send, x_recv, ab * D) for ab in range(4)]

    def weights_cross(n):
        wc[n][0].start()

    def weights_turn(n):
        wc[n][0].wait_recv()
        for i in (1, 2, 3):
            wc[n][i].start()

    def weights_forward(n):
        wc[n][1].wait_recv()
        wc[n][4].start()
        wc[n][5].start()
        wc[n][2].wait_recv()
        wc[n][6].start()
        wc[n][7].start()

    def weights_last(n):
        wc[n][4].wait_recv()
        wc[n][8].start()
        wc[n][6].wait_recv()
        wc[n][9].start()

    def weights_here(n):
        for i in (3, 5, 7, 8, 9):
            wc[n][i].wait_recv()

    norm(0, 32)
    norm(32, 32)
    norm(64, 32)
    pl.semaphore_wait(barrier, 11)
    weights_cross(0)
    for i in (0, 1, 2):
        gc[i].start()
    norm(96, 32)
    for i in (3, 4, 5):
        gc[i].start()
    for c in w_copies:
        c.wait()

    def after(done, *then):
        gc[done].wait_recv()
        for i in then:
            gc[i].start()

    def project_qk(g):
        x = xg[2 * g : 2 * g + 2].reshape(2 * CH, D)
        rows = pl.ds(2 * g * CH, 2 * CH)
        for j in range(2):
            part = jnp.dot(x, w[j], preferred_element_type=F32)
            qk[j, rows] = part
            for u in range(2):
                p = part[u * CH : (u + 1) * CH]
                sq = p * p
                sq = sq[:, :HD] + sq[:, HD : 2 * HD] + sq[:, 2 * HD :]
                row = jnp.sum(jnp.transpose(sq), axis=0, keepdims=True)
                sums[t, chunk_of[2 * g + u], :, j * HD : (j + 1) * HD] = row

    def project_v(g):
        x = xg[2 * g : 2 * g + 2].reshape(2 * CH, D)
        part = jnp.dot(x, w[2], preferred_element_type=F32).astype(BF16)
        for h in range(LH):
            v[h, pl.ds(2 * g * CH, 2 * CH), :HD] = part[:, h * HD : (h + 1) * HD]

    after(1, 6)
    after(2, 7)
    after(0, 8, 9)
    after(3, 12, 14)
    after(4, 13, 15)
    after(5)
    project_qk(0)
    project_v(0)
    weights_turn(0)
    after(8, 10)
    after(9, 11)
    after(12, 16)
    after(13, 17)
    weights_cross(1)
    project_qk(1)
    project_v(1)
    v[:, :, HD:] = jnp.ones((LH, 8 * CH, HD), BF16)
    weights_forward(0)
    after(14)
    after(15)
    project_qk(2)
    project_v(2)
    weights_last(0)
    for i in (6, 7, 16, 17, 10, 11):
        after(i)
    weights_cross(2)
    project_qk(3)

    s_copies = [
        remote(sums.at[t], sums.at[t], s_send.at[n], s_recv.at[n], {"tensor": lax.rem(t + n, 8)}) for n in range(1, 8)
    ]
    for c in gc:
        c.wait_send()
    for c in s_copies:
        c.start()
    project_v(3)
    weights_turn(1)
    for n in range(1, 8):
        there = sums.at[lax.rem(t + 8 - n, 8)]
        remote(there, there, s_send.at[n], s_recv.at[n], {"tensor": lax.rem(t + n, 8)}).wait_recv()
    def scale(slot, j):
        total = sums[0, chunk_of[slot], :, j * HD : (j + 1) * HD]
        for other in range(1, 8):
            total = total + sums[other, chunk_of[slot], :, j * HD : (j + 1) * HD]
        factor = lax.rsqrt(total / (HEADS * HD) + EPS)
        out, gains, extra = ((q, q_gain, HD**-0.5 * LOG2E), (k, k_gain, 1.0))[j]
        col = jnp.transpose(jnp.broadcast_to(factor, (CH, HD))) * extra
        gains = gains[...].reshape(1, LW)
        for h in range(LH):
            lanes = slice(h * HD, (h + 1) * HD)
            out[h, pl.ds(slot * CH, CH)] = (qk[j, pl.ds(slot * CH, CH), lanes] * col * gains[:, lanes]).astype(BF16)

    for slot in range(8):
        scale(slot, 1)

    def attend(slot, *places):
        scale(slot, 0)
        scale(slot + 1, 0)

        def one(h, _):
            rows = pl.ds(slot * CH, 2 * CH)
            scores = lax.dot_general(q[h, rows], k[h], (((1,), (1,)), ((), ())), preferred_element_type=F32)
            e = jnp.exp2(scores - jnp.max(scores, axis=-1, keepdims=True)).astype(BF16)
            part = jnp.dot(e, v[h], preferred_element_type=F32)
            part = (part[:, :HD] / part[:, HD:]).astype(BF16)
            lanes = pl.ds(pl.multiple_of(h * HD, HD), HD)
            for n, (dst, place) in enumerate(places):
                dst[place, :, lanes] = part[n * CH : (n + 1) * CH]
            return _

        lax.fori_loop(0, LH, one, 0)

    mc = [remote(far.at[n], mix.at[1, n], m_send.at[n], m_recv.at[n], directions()["x"]) for n in range(4)]
    rc = [
        remote(ob.at[src, pl.ds(row, 32)], xg.at[4 + i // 4, pl.ds(32 * (i % 4), 32)], r_send.at[i], r_recv.at[i], directions()[way])
        for i, (src, row, way, _) in enumerate(SCATTER)
    ]
    ec = table_copies(SPREAD, xg, e_send, e_recv)

    def branch(n, count):
        for i in range(n, n + count):
            mc[i].wait_recv()
        x = jnp.concatenate([mix[c, n : n + count].reshape(count * CH, LW) for c in range(2)], axis=1)
        for n0 in range(0, D, 1280):
            cols = slice(n0, min(n0 + 1280, D))
            part = jnp.dot(x, wo[:, cols], preferred_element_type=F32).astype(BF16)
            for i in range(count):
                ob[n + i, :, cols] = part[i * CH : (i + 1) * CH]

    def add(i):
        rc[i].wait_recv()
        _, row, _, dst = SCATTER[i]
        total = ob[dst, row : row + 32].astype(F32) + xg[4 + i // 4, 32 * (i % 4) : 32 * (i % 4) + 32].astype(F32)
        ob[dst, row : row + 32] = total.astype(BF16)

    own, off = mix.at[0], far
    attend(O2, (own, N2), (off, N2))
    mc[N2].start()
    attend(X1, (off, N1), (off, NM))
    mc[N1].start()
    mc[NM].start()
    own_copies[0].wait()
    weights_here(0)
    branch(N2, 1)
    for i in (0, 1, 6, 7):
        rc[i].start()
    attend(O1, (own, N1), (own, NM))
    branch(N1, 2)
    for i in (2, 4):
        rc[i].start()
    weights_turn(2)
    weights_cross(3)
    attend(O0, (own, N0), (off, N0))
    mc[N0].start()
    add(0)
    rc[3].start()
    add(1)
    rc[5].start()
    for i in (8, 10):
        rc[i].start()
    weights_forward(1)
    branch(N0, 1)
    weights_cross(4)
    add(6)
    rc[9].start()
    add(7)
    rc[11].start()
    weights_turn(3)

    def encode(row0):
        base = jnp.dot(merge_order(row0, 32), patches[...], preferred_element_type=F32)
        total = ob[N0, row0 : row0 + 32].astype(F32)
        xg[N0, pl.ds(row0, 32)] = (base + layer_scale[...].reshape(1, D) * total).astype(BF16)

    def encode_half(half):
        for i in (2, 4, 3, 5):
            add(6 * half + i)
        encode(64 * half)
        encode(64 * half + 32)
        ec[4 * half].start()
        ec[4 * half + 1].start()

    encode_half(0)
    weights_last(1)
    weights_forward(2)
    weights_turn(4)
    encode_half(1)
    weights_forward(3)
    weights_last(2)
    for c in rc + mc:
        c.wait_send()

    def forward(half):
        ec[4 * half].wait_recv()
        ec[4 * half + 2].start()
        ec[4 * half + 1].wait_recv()
        ec[4 * half + 3].start()

    def project(ab, c):
        x = xg[0:4, ab * 32 : (ab + 1) * 32, :].reshape(4 * 32, D)
        return jnp.dot(x, wp[c, ab * D : (ab + 1) * D, :], preferred_element_type=F32)

    forward(0)
    weights_forward(4)
    weights_last(3)
    forward(1)
    own_copies[1].wait()
    ec[2].wait_recv()
    ec[3].wait_recv()
    weights_here(1)
    weights_here(2)
    early = [project(0, c) + project(1, c) for c in range(2)]
    weights_last(4)
    ec[6].wait_recv()
    ec[7].wait_recv()
    weights_here(3)
    weights_here(4)

    mine = me // 8 == xh

    def piece_copy(n, c):
        m = lax.rem(me + n, 8)
        target = group(8 * xh + m, (t, opp)[c])
        return remote(proj.at[c, m], pieces.at[me], a_send.at[c, n], a_recv.at[me], target)

    def first_copies(c, act):
        for n in range(1, 8):
            act(piece_copy(n, c))
        if c:
            act(piece_copy(0, 1))
        else:

            @pl.when(jnp.logical_not(mine))
            def _():
                act(piece_copy(0, 0))

    for c in range(2):
        out = (early[c] + project(2, c) + project(3, c)).astype(BF16)
        for n, slot in ((N2, O2), (N1, O1), (NM, OM), (N0, O0)):
            place = 2 * lax.rem(chunk_of[slot], 4)
            proj[c, pl.ds(place, 2)] = out[n * 32 : (n + 1) * 32].reshape(2, 16, 512)
        first_copies(c, lambda copy: copy.start())

    @pl.when(mine)
    def _():
        pieces[me] = proj[0, lax.rem(me, 8)]

    def piece_here(g):
        remote(pieces.at[g], pieces.at[g], a_send.at[0, 0], a_recv.at[g], group(me, opp)).wait_recv()

    for n in range(1, 16):
        piece_here(lax.rem(me + n, 16))

    @pl.when(jnp.logical_not(mine))
    def _():
        piece_here(me)

    start = jnp.int32(0)
    for g in range(16):
        for s in range(2):
            tile = slots[jnp.minimum(start + s, 15)]
            picked[g, s] = pieces[tile]
        start = start + counts[g]
    second = [
        remote(
            picked.at[lax.rem(me + n, 16)], arrive.at[me], b_send.at[n], b_recv.at[n], group(lax.rem(me + n, 16), t)
        )
        for n in range(1, 16)
    ]
    for c in second:
        c.start()
    arrive[me] = picked[me]
    for n in range(1, 16):
        there = arrive.at[lax.rem(me + 16 - n, 16)]
        remote(there, there, b_send.at[n], b_recv.at[n], group(lax.rem(me + n, 16), t)).wait_recv()
    for n in range(16):
        for s in range(2):
            feats[s * 256 + n * 16 : s * 256 + n * 16 + 16, :] = arrive[n, s]
    for c in range(2):
        first_copies(c, lambda copy: copy.wait_send())
    for c in s_copies + second + ec + [c for copies in wc for c in copies]:
        c.wait_send()


def place_kernel(feats, text_hbm, counts, offsets, out, text, sem):
    copy = pltpu.make_async_copy(text_hbm, text, sem)
    copy.start()
    me = lax.axis_index("section") * 2 + lax.axis_index("dp")
    rows = counts[me] * 256
    offset = offsets[me]
    seq = text.shape[0]
    r = lax.broadcasted_iota(jnp.int32, (seq, 512), 0) - offset
    c = lax.broadcasted_iota(jnp.int32, (seq, 512), 1)
    pick = (r == c).astype(F32).astype(BF16)
    moved = jnp.dot(pick, feats[...], preferred_element_type=F32).astype(BF16)
    copy.wait()
    out[...] = jnp.where((r >= 0) & (r < rows), moved, text[...])


def spec(space):
    return pl.BlockSpec(memory_space=space)


def shards(
    patches,
    norm_gain,
    w_qkv,
    q_gain,
    k_gain,
    w_out,
    layer_scale,
    w_proj,
    text_embed,
    tile_counts,
    image_offsets,
    tile_slots,
):
    dma = pltpu.SemaphoreType.DMA
    smem = pltpu.SMEM
    heads = VMEM((LH, 8 * CH, HD), BF16)
    values = VMEM((LH, 8 * CH, 2 * HD), BF16)
    feats = pl.pallas_call(
        encode_kernel,
        out_shape=jax.ShapeDtypeStruct((512, 512), BF16),
        in_specs=[spec(s) for s in (VMEM, VMEM, pl.ANY, VMEM, VMEM, VMEM, pl.ANY, pl.ANY, smem, smem)],
        out_specs=spec(VMEM),
        scratch_shapes=[
            VMEM((8, CH, D), BF16),
            VMEM((3, D, LW), BF16),
            VMEM((2, 8 * CH, LW), F32),
            VMEM((8, 8, 1, 2 * HD), F32),
            heads,
            heads,
            values,
            VMEM((2 * LW, D), BF16),
            VMEM((2, 4 * D, 512), BF16),
            VMEM((2, 4, CH, LW), BF16),
            VMEM((4, CH, LW), BF16),
            VMEM((4, CH, D), BF16),
            VMEM((2, 8, 16, 512), BF16),
            VMEM((16, 16, 512), BF16),
            VMEM((16, 2, 16, 512), BF16),
            VMEM((16, 2, 16, 512), BF16),
            dma((5,)),
            dma((len(GATHER),)),
            dma((len(GATHER),)),
            dma((8,)),
            dma((8,)),
            dma((len(SETS), 10)),
            dma((len(SETS), 10)),
            dma((4,)),
            dma((4,)),
            dma((len(SCATTER),)),
            dma((len(SCATTER),)),
            dma((len(SPREAD),)),
            dma((len(SPREAD),)),
            dma((2, 8)),
            dma((16,)),
            dma((16,)),
            dma((16,)),
        ],
        compiler_params=pltpu.CompilerParams(collective_id=0, **PARAMS),
        name="encode",
    )(
        patches[0],
        norm_gain,
        w_qkv.transpose(1, 0, 2),
        q_gain,
        k_gain,
        layer_scale,
        w_out,
        w_proj,
        tile_counts,
        tile_slots,
    )
    out = pl.pallas_call(
        place_kernel,
        out_shape=jax.ShapeDtypeStruct(text_embed.shape[1:], BF16),
        in_specs=[spec(s) for s in (VMEM, pl.ANY, smem, smem)],
        out_specs=spec(VMEM),
        scratch_shapes=[VMEM(text_embed.shape[1:], BF16), pltpu.SemaphoreType.DMA],
        compiler_params=pltpu.CompilerParams(vmem_limit_bytes=62 * 1024 * 1024),
        name="place",
    )(feats, text_embed[0], tile_counts, image_offsets)
    return out[None]


def solution(mesh):
    placed = (
        P(("section", "dp"), "tensor", None),
        P(),
        P(None, None, "tensor"),
        P("tensor"),
        P("tensor"),
        P("tensor", None),
        P(),
        P(None, "tensor"),
        P(("section", "dp"), None, "tensor"),
        P(),
        P(),
        P(),
    )
    return jax.shard_map(
        shards,
        mesh=mesh,
        in_specs=placed,
        out_specs=P(("section", "dp"), None, "tensor"),
        check_vma=False,
    )
```

```python
import jax
import jax.numpy as jnp
from jax import lax
from jax.experimental import pallas as pl
from jax.experimental.pallas import tpu as pltpu
from jax.sharding import PartitionSpec as P

D = 3200
HEADS = 24
HD = 128
CH = 128
LH = 3
LW = 384
F32 = jnp.float32
BF16 = jnp.bfloat16
MESH = pl.DeviceIdType.MESH
EPS = 1e-06
LOG2E = 1.4426950408889634
VMEM = pltpu.VMEM
PARAMS = dict(has_side_effects=True, vmem_limit_bytes=62 * 1024 * 1024)

O0, X0, O1, OM, X1, XM, O2, X2 = range(8)
N2, N1, NM, N0 = range(4)

GATHER = (
    (O0, 0, 96, "x", X0),
    (O0, 0, 96, "p", OM),
    (O0, 0, 96, "m", O1),
    (O0, 96, 32, "p", OM),
    (O0, 96, 32, "m", O1),
    (O0, 96, 32, "x", X0),
    (OM, 0, 48, "p", O2),
    (O1, 48, 48, "m", O2),
    (X0, 0, 96, "p", XM),
    (X0, 0, 96, "m", X1),
    (XM, 0, 48, "p", X2),
    (X1, 48, 48, "m", X2),
    (OM, 96, 16, "p", O2),
    (O1, 112, 16, "m", O2),
    (OM, 96, 32, "x", XM),
    (O1, 96, 32, "x", X1),
    (O2, 96, 16, "x", X2),
    (O2, 112, 16, "x", X2),
)

SCATTER = tuple(
    copy
    for b in (0, 64)
    for copy in (
        (N2, b, "p", N1),
        (N2, b + 32, "m", NM),
        (N1, b + 32, "p", N0),
        (N1, b, "p", N0),
        (NM, b, "m", N0),
        (NM, b + 32, "m", N0),
    )
)

SPREAD = tuple(
    copy
    for b in (0, 64)
    for copy in ((N0, b, 64, "p", NM), (N0, b, 64, "m", N1), (NM, b, 32, "p", N2), (N1, b + 32, 32, "m", N2))
)

SETS = ((48, 32), (400, 208), (400, 208), (400, 208), (400, 208))
WEIGHTS = ((0, 0, "u"), (0, 0, "d"), (0, 0, "c"), (-2, 1, "u"), (-2, 0, "c"), (2, 2, "d"), (2, 0, "c"), (4, 1, "c"), (4, 2, "c"))


def where_am_i():
    t = lax.axis_index("tensor")
    return t, t // 4, lax.rem(t, 4)


def directions():
    _, xh, y = where_am_i()
    section = lax.axis_index("section")
    return {
        "p": {"tensor": xh * 4 + lax.rem(y + 1, 4)},
        "m": {"tensor": xh * 4 + lax.rem(y + 3, 4)},
        "x": {"tensor": (1 - xh) * 4 + y},
        "cross": {"dp": 1 - lax.axis_index("dp"), "tensor": (1 - xh) * 4 + y},
        "u": {"section": lax.rem(section + 2, 8)},
        "d": {"section": lax.rem(section + 6, 8)},
        "c": {"section": section + 1 - 2 * lax.rem(section, 2)},
    }


def slot_chunks():
    _, xh, y = where_am_i()
    near, far = xh * 4, (1 - xh) * 4
    up, down, opposite = lax.rem(y + 1, 4), lax.rem(y + 3, 4), lax.rem(y + 2, 4)
    return (near + y, far + y, near + up, near + down, far + up, far + down, near + opposite, far + opposite)


def remote(src, dst, send, recv, target):
    return pltpu.make_async_remote_copy(
        src_ref=src, dst_ref=dst, send_sem=send, recv_sem=recv, device_id=target, device_id_type=MESH
    )


def table_copies(table, buf, send, recv):
    where = directions()
    return [
        remote(buf.at[src, pl.ds(row, rows)], buf.at[dst, pl.ds(row, rows)], send.at[i], recv.at[i], where[way])
        for i, (src, row, rows, way, dst) in enumerate(table)
    ]


def weight_copies(number, source, buf, base, send, recv, source_base=0):
    rows, first = SETS[number]
    section = lax.axis_index("section")
    where = directions()

    def part(ref, offset, which, base=base):
        start = base + lax.rem(section + 8 + offset, 8) * rows
        start, count = ((start, rows), (start, first), (start + first, rows - first))[which]
        return ref.at[pl.ds(pl.multiple_of(start, 16), count)]

    copies = [remote(part(source, 0, 0, source_base), part(buf, 0, 0), send.at[number, 0], recv.at[number, 0], where["cross"])]
    for i, (offset, which, way) in enumerate(WEIGHTS):
        there = part(buf, offset, which)
        copies.append(remote(there, there, send.at[number, i + 1], recv.at[number, i + 1], where[way]))
    return copies


def merge_order(row0, rows):
    r = lax.broadcasted_iota(jnp.int32, (rows, CH), 0) + row0
    c = lax.broadcasted_iota(jnp.int32, (rows, CH), 1)
    a, b, i, j = r // 64, (r // 32) % 2, (r // 16) % 2, r % 16
    return ((2 * i + a) * 32 + 2 * j + b == c).astype(F32).astype(BF16)


def encode_kernel(
    patches, gain, w_hbm, q_gain, k_gain, layer_scale, wo_hbm, wp_hbm, counts, slots, feats,
    xg, w, qk, sums, q, k, v, wo, wp, mix, far, ob, proj, pieces, picked, arrive,
    w_sem, g_send, g_recv, s_send, s_recv, x_send, x_recv, m_send, m_recv, r_send, r_recv, e_send, e_recv,
    a_send, a_recv, b_send, b_recv,
):
    t, xh, y = where_am_i()
    opp = (1 - xh) * 4 + y
    chunk_of = slot_chunks()
    me = lax.axis_index("section") * 2 + lax.axis_index("dp")

    def group(index, tensor):
        return {"section": index // 2, "dp": lax.rem(index, 2), "tensor": tensor}

    w_copies = [pltpu.make_async_copy(w_hbm.at[j], w.at[j], w_sem.at[j]) for j in range(3)]
    own_copies = [
        pltpu.make_async_copy(wo_hbm, wo.at[pl.ds(0, LW)], w_sem.at[3]),
        pltpu.make_async_copy(wp_hbm, wp.at[0], w_sem.at[4]),
    ]
    for c in w_copies + own_copies:
        c.start()
    barrier = pltpu.get_barrier_semaphore()
    for n in range(1, 8):
        pl.semaphore_signal(barrier, inc=1, device_id={"tensor": lax.rem(t + n, 8)}, device_id_type=MESH)
    for way in ("cross", "u", "d", "c"):
        pl.semaphore_signal(barrier, inc=1, device_id=directions()[way], device_id_type=MESH)

    def norm(row0, rows):
        x = jnp.dot(merge_order(row0, rows), patches[...], preferred_element_type=F32)
        scale = lax.rsqrt(jnp.mean(x * x, axis=-1, keepdims=True) + EPS)
        xg[O0, pl.ds(row0, rows)] = (x * scale * gain[...].reshape(1, D)).astype(BF16)

    gc = table_copies(GATHER, xg, g_send, g_recv)
    wc = [weight_copies(0, wo_hbm, wo, LW, x_send, x_recv)]
    wc += [weight_copies(1 + ab, wp_hbm, wp.at[1], ab * D, x_send, x_recv, ab * D) for ab in range(4)]

    def weights_cross(n):
        wc[n][0].start()

    def weights_turn(n):
        wc[n][0].wait_recv()
        for i in (1, 2, 3):
            wc[n][i].start()

    def weights_forward(n):
        wc[n][1].wait_recv()
        wc[n][4].start()
        wc[n][5].start()
        wc[n][2].wait_recv()
        wc[n][6].start()
        wc[n][7].start()

    def weights_last(n):
        wc[n][4].wait_recv()
        wc[n][8].start()
        wc[n][6].wait_recv()
        wc[n][9].start()

    def weights_here(n):
        for i in (3, 5, 7, 8, 9):
            wc[n][i].wait_recv()

    norm(0, 32)
    norm(32, 32)
    norm(64, 32)
    pl.semaphore_wait(barrier, 11)
    weights_cross(0)
    for i in (0, 1, 2):
        gc[i].start()
    norm(96, 32)
    for i in (3, 4, 5):
        gc[i].start()
    for c in w_copies:
        c.wait()

    def after(done, *then):
        gc[done].wait_recv()
        for i in then:
            gc[i].start()

    def project_qk(g):
        x = xg[2 * g : 2 * g + 2].reshape(2 * CH, D)
        rows = pl.ds(2 * g * CH, 2 * CH)
        for j in range(2):
            part = jnp.dot(x, w[j], preferred_element_type=F32)
            qk[j, rows] = part
            for u in range(2):
                p = part[u * CH : (u + 1) * CH]
                sq = p * p
                sq = sq[:, :HD] + sq[:, HD : 2 * HD] + sq[:, 2 * HD :]
                row = jnp.sum(jnp.transpose(sq), axis=0, keepdims=True)
                sums[t, chunk_of[2 * g + u], :, j * HD : (j + 1) * HD] = row

    def project_v(g):
        x = xg[2 * g : 2 * g + 2].reshape(2 * CH, D)
        part = jnp.dot(x, w[2], preferred_element_type=F32).astype(BF16)
        for h in range(LH):
            v[h, pl.ds(2 * g * CH, 2 * CH), :HD] = part[:, h * HD : (h + 1) * HD]

    after(1, 6)
    after(2, 7)
    after(0, 8, 9)
    after(3, 12, 14)
    after(4, 13, 15)
    after(5)
    project_qk(0)
    project_v(0)
    weights_turn(0)
    after(8, 10)
    after(9, 11)
    after(12, 16)
    after(13, 17)
    weights_cross(1)
    project_qk(1)
    project_v(1)
    v[:, :, HD:] = jnp.ones((LH, 8 * CH, HD), BF16)
    weights_forward(0)
    after(14)
    after(15)
    project_qk(2)
    project_v(2)
    weights_last(0)
    for i in (6, 7, 16, 17, 10, 11):
        after(i)
    weights_cross(2)
    project_qk(3)

    s_copies = [
        remote(sums.at[t], sums.at[t], s_send.at[n], s_recv.at[n], {"tensor": lax.rem(t + n, 8)}) for n in range(1, 8)
    ]
    for c in gc:
        c.wait_send()
    for c in s_copies:
        c.start()
    project_v(3)
    weights_turn(1)
    for n in range(1, 8):
        there = sums.at[lax.rem(t + 8 - n, 8)]
        remote(there, there, s_send.at[n], s_recv.at[n], {"tensor": lax.rem(t + n, 8)}).wait_recv()
    def scale(slot, j):
        total = sums[0, chunk_of[slot], :, j * HD : (j + 1) * HD]
        for other in range(1, 8):
            total = total + sums[other, chunk_of[slot], :, j * HD : (j + 1) * HD]
        factor = lax.rsqrt(total / (HEADS * HD) + EPS)
        out, gains, extra = ((q, q_gain, HD**-0.5 * LOG2E), (k, k_gain, 1.0))[j]
        col = jnp.transpose(jnp.broadcast_to(factor, (CH, HD))) * extra
        gains = gains[...].reshape(1, LW)
        for h in range(LH):
            lanes = slice(h * HD, (h + 1) * HD)
            out[h, pl.ds(slot * CH, CH)] = (qk[j, pl.ds(slot * CH, CH), lanes] * col * gains[:, lanes]).astype(BF16)

    for slot in range(8):
        scale(slot, 1)

    def attend(slot, *places):
        scale(slot, 0)
        scale(slot + 1, 0)

        def one(h, _):
            rows = pl.ds(slot * CH, 2 * CH)
            scores = lax.dot_general(q[h, rows], k[h], (((1,), (1,)), ((), ())), preferred_element_type=F32)
            e = jnp.exp2(scores - jnp.max(scores, axis=-1, keepdims=True)).astype(BF16)
            part = jnp.dot(e, v[h], preferred_element_type=F32)
            part = (part[:, :HD] / part[:, HD:]).astype(BF16)
            lanes = pl.ds(pl.multiple_of(h * HD, HD), HD)
            for n, (dst, place) in enumerate(places):
                dst[place, :, lanes] = part[n * CH : (n + 1) * CH]
            return _

        lax.fori_loop(0, LH, one, 0)

    mc = [remote(far.at[n], mix.at[1, n], m_send.at[n], m_recv.at[n], directions()["x"]) for n in range(4)]
    rc = [
        remote(ob.at[src, pl.ds(row, 32)], xg.at[4 + i // 4, pl.ds(32 * (i % 4), 32)], r_send.at[i], r_recv.at[i], directions()[way])
        for i, (src, row, way, _) in enumerate(SCATTER)
    ]
    ec = table_copies(SPREAD, xg, e_send, e_recv)

    def branch(n, count):
        for i in range(n, n + count):
            mc[i].wait_recv()
        x = jnp.concatenate([mix[c, n : n + count].reshape(count * CH, LW) for c in range(2)], axis=1)
        for n0 in range(0, D, 1280):
            cols = slice(n0, min(n0 + 1280, D))
            part = jnp.dot(x, wo[:, cols], preferred_element_type=F32).astype(BF16)
            for i in range(count):
                ob[n + i, :, cols] = part[i * CH : (i + 1) * CH]

    def add(i):
        rc[i].wait_recv()
        _, row, _, dst = SCATTER[i]
        total = ob[dst, row : row + 32].astype(F32) + xg[4 + i // 4, 32 * (i % 4) : 32 * (i % 4) + 32].astype(F32)
        ob[dst, row : row + 32] = total.astype(BF16)

    own, off = mix.at[0], far
    attend(O2, (own, N2), (off, N2))
    mc[N2].start()
    attend(X1, (off, N1), (off, NM))
    mc[N1].start()
    mc[NM].start()
    own_copies[0].wait()
    weights_here(0)
    branch(N2, 1)
    for i in (0, 1, 6, 7):
        rc[i].start()
    attend(O1, (own, N1), (own, NM))
    branch(N1, 2)
    for i in (2, 4):
        rc[i].start()
    weights_turn(2)
    weights_cross(3)
    attend(O0, (own, N0), (off, N0))
    mc[N0].start()
    add(0)
    rc[3].start()
    add(1)
    rc[5].start()
    for i in (8, 10):
        rc[i].start()
    branch(N0, 1)
    weights_cross(4)
    add(6)
    rc[9].start()
    add(7)
    rc[11].start()
    weights_forward(1)
    weights_turn(3)

    def encode(row0):
        base = jnp.dot(merge_order(row0, 32), patches[...], preferred_element_type=F32)
        total = ob[N0, row0 : row0 + 32].astype(F32)
        xg[N0, pl.ds(row0, 32)] = (base + layer_scale[...].reshape(1, D) * total).astype(BF16)

    def encode_half(half):
        for i in (2, 4, 3, 5):
            add(6 * half + i)
        encode(64 * half)
        encode(64 * half + 32)
        ec[4 * half].start()
        ec[4 * half + 1].start()

    encode_half(0)
    weights_last(1)
    weights_forward(2)
    weights_turn(4)
    encode_half(1)
    weights_forward(3)
    weights_last(2)
    for c in rc + mc:
        c.wait_send()

    def forward(half):
        ec[4 * half].wait_recv()
        ec[4 * half + 2].start()
        ec[4 * half + 1].wait_recv()
        ec[4 * half + 3].start()

    def project(ab, c):
        x = xg[0:4, ab * 32 : (ab + 1) * 32, :].reshape(4 * 32, D)
        return jnp.dot(x, wp[c, ab * D : (ab + 1) * D, :], preferred_element_type=F32)

    forward(0)
    forward(1)
    weights_forward(4)
    weights_last(3)
    own_copies[1].wait()
    ec[2].wait_recv()
    ec[3].wait_recv()
    weights_here(1)
    weights_here(2)
    early = [project(0, c) + project(1, c) for c in range(2)]
    weights_last(4)
    ec[6].wait_recv()
    ec[7].wait_recv()
    weights_here(3)
    weights_here(4)

    mine = me // 8 == xh

    def piece_copy(n, c):
        m = lax.rem(me + n, 8)
        target = group(8 * xh + m, (t, opp)[c])
        return remote(proj.at[c, m], pieces.at[me], a_send.at[c, n], a_recv.at[me], target)

    def first_copies(c, act):
        for n in range(1, 8):
            act(piece_copy(n, c))
        if c:
            act(piece_copy(0, 1))
        else:

            @pl.when(jnp.logical_not(mine))
            def _():
                act(piece_copy(0, 0))

    for c in range(2):
        out = (early[c] + project(2, c) + project(3, c)).astype(BF16)
        for n, slot in ((N2, O2), (N1, O1), (NM, OM), (N0, O0)):
            place = 2 * lax.rem(chunk_of[slot], 4)
            proj[c, pl.ds(place, 2)] = out[n * 32 : (n + 1) * 32].reshape(2, 16, 512)
        first_copies(c, lambda copy: copy.start())

    @pl.when(mine)
    def _():
        pieces[me] = proj[0, lax.rem(me, 8)]

    def piece_here(g):
        remote(pieces.at[g], pieces.at[g], a_send.at[0, 0], a_recv.at[g], group(me, opp)).wait_recv()

    for n in range(1, 16):
        piece_here(lax.rem(me + n, 16))

    @pl.when(jnp.logical_not(mine))
    def _():
        piece_here(me)

    start = jnp.int32(0)
    for g in range(16):
        for s in range(2):
            tile = slots[jnp.minimum(start + s, 15)]
            picked[g, s] = pieces[tile]
        start = start + counts[g]
    second = [
        remote(
            picked.at[lax.rem(me + n, 16)], arrive.at[me], b_send.at[n], b_recv.at[n], group(lax.rem(me + n, 16), t)
        )
        for n in range(1, 16)
    ]
    for c in second:
        c.start()
    arrive[me] = picked[me]
    for n in range(1, 16):
        there = arrive.at[lax.rem(me + 16 - n, 16)]
        remote(there, there, b_send.at[n], b_recv.at[n], group(lax.rem(me + n, 16), t)).wait_recv()
    for n in range(16):
        for s in range(2):
            feats[s * 256 + n * 16 : s * 256 + n * 16 + 16, :] = arrive[n, s]
    for c in range(2):
        first_copies(c, lambda copy: copy.wait_send())
    for c in s_copies + second + ec + [c for copies in wc for c in copies]:
        c.wait_send()


def place_kernel(feats, text_hbm, counts, offsets, out, text, sem):
    copy = pltpu.make_async_copy(text_hbm, text, sem)
    copy.start()
    me = lax.axis_index("section") * 2 + lax.axis_index("dp")
    rows = counts[me] * 256
    offset = offsets[me]
    seq = text.shape[0]
    r = lax.broadcasted_iota(jnp.int32, (seq, 512), 0) - offset
    c = lax.broadcasted_iota(jnp.int32, (seq, 512), 1)
    pick = (r == c).astype(F32).astype(BF16)
    moved = jnp.dot(pick, feats[...], preferred_element_type=F32).astype(BF16)
    copy.wait()
    out[...] = jnp.where((r >= 0) & (r < rows), moved, text[...])


def spec(space):
    return pl.BlockSpec(memory_space=space)


def shards(
    patches,
    norm_gain,
    w_qkv,
    q_gain,
    k_gain,
    w_out,
    layer_scale,
    w_proj,
    text_embed,
    tile_counts,
    image_offsets,
    tile_slots,
):
    dma = pltpu.SemaphoreType.DMA
    smem = pltpu.SMEM
    heads = VMEM((LH, 8 * CH, HD), BF16)
    values = VMEM((LH, 8 * CH, 2 * HD), BF16)
    feats = pl.pallas_call(
        encode_kernel,
        out_shape=jax.ShapeDtypeStruct((512, 512), BF16),
        in_specs=[spec(s) for s in (VMEM, VMEM, pl.ANY, VMEM, VMEM, VMEM, pl.ANY, pl.ANY, smem, smem)],
        out_specs=spec(VMEM),
        scratch_shapes=[
            VMEM((8, CH, D), BF16),
            VMEM((3, D, LW), BF16),
            VMEM((2, 8 * CH, LW), F32),
            VMEM((8, 8, 1, 2 * HD), F32),
            heads,
            heads,
            values,
            VMEM((2 * LW, D), BF16),
            VMEM((2, 4 * D, 512), BF16),
            VMEM((2, 4, CH, LW), BF16),
            VMEM((4, CH, LW), BF16),
            VMEM((4, CH, D), BF16),
            VMEM((2, 8, 16, 512), BF16),
            VMEM((16, 16, 512), BF16),
            VMEM((16, 2, 16, 512), BF16),
            VMEM((16, 2, 16, 512), BF16),
            dma((5,)),
            dma((len(GATHER),)),
            dma((len(GATHER),)),
            dma((8,)),
            dma((8,)),
            dma((len(SETS), 10)),
            dma((len(SETS), 10)),
            dma((4,)),
            dma((4,)),
            dma((len(SCATTER),)),
            dma((len(SCATTER),)),
            dma((len(SPREAD),)),
            dma((len(SPREAD),)),
            dma((2, 8)),
            dma((16,)),
            dma((16,)),
            dma((16,)),
        ],
        compiler_params=pltpu.CompilerParams(collective_id=0, **PARAMS),
        name="encode",
    )(
        patches[0],
        norm_gain,
        w_qkv.transpose(1, 0, 2),
        q_gain,
        k_gain,
        layer_scale,
        w_out,
        w_proj,
        tile_counts,
        tile_slots,
    )
    out = pl.pallas_call(
        place_kernel,
        out_shape=jax.ShapeDtypeStruct(text_embed.shape[1:], BF16),
        in_specs=[spec(s) for s in (VMEM, pl.ANY, smem, smem)],
        out_specs=spec(VMEM),
        scratch_shapes=[VMEM(text_embed.shape[1:], BF16), pltpu.SemaphoreType.DMA],
        compiler_params=pltpu.CompilerParams(vmem_limit_bytes=62 * 1024 * 1024),
        name="place",
    )(feats, text_embed[0], tile_counts, image_offsets)
    return out[None]


def solution(mesh):
    placed = (
        P(("section", "dp"), "tensor", None),
        P(),
        P(None, None, "tensor"),
        P("tensor"),
        P("tensor"),
        P("tensor", None),
        P(),
        P(None, "tensor"),
        P(("section", "dp"), None, "tensor"),
        P(),
        P(),
        P(),
    )
    return jax.shard_map(
        shards,
        mesh=mesh,
        in_specs=placed,
        out_specs=P(("section", "dp"), None, "tensor"),
        check_vma=False,
    )
```

```python
import jax
import jax.numpy as jnp
from jax import lax
from jax.experimental import pallas as pl
from jax.experimental.pallas import tpu as pltpu
from jax.sharding import PartitionSpec as P

D = 3200
HEADS = 24
HD = 128
CH = 128
LH = 3
LW = 384
F32 = jnp.float32
BF16 = jnp.bfloat16
MESH = pl.DeviceIdType.MESH
EPS = 1e-06
LOG2E = 1.4426950408889634
VMEM = pltpu.VMEM
PARAMS = dict(has_side_effects=True, vmem_limit_bytes=62 * 1024 * 1024)

O0, X0, O1, OM, X1, XM, O2, X2 = range(8)
N2, N1, NM, N0 = range(4)

GATHER = (
    (O0, 0, 96, "x", X0),
    (O0, 0, 96, "p", OM),
    (O0, 0, 96, "m", O1),
    (O0, 96, 32, "p", OM),
    (O0, 96, 32, "m", O1),
    (O0, 96, 32, "x", X0),
    (OM, 0, 48, "p", O2),
    (O1, 48, 48, "m", O2),
    (X0, 0, 96, "p", XM),
    (X0, 0, 96, "m", X1),
    (XM, 0, 48, "p", X2),
    (X1, 48, 48, "m", X2),
    (OM, 96, 16, "p", O2),
    (O1, 112, 16, "m", O2),
    (OM, 96, 32, "x", XM),
    (O1, 96, 32, "x", X1),
    (O2, 96, 16, "x", X2),
    (O2, 112, 16, "x", X2),
)

SCATTER = tuple(
    copy
    for b in (0, 64)
    for copy in (
        (N2, b, "p", N1),
        (N2, b + 32, "m", NM),
        (N1, b + 32, "p", N0),
        (N1, b, "p", N0),
        (NM, b, "m", N0),
        (NM, b + 32, "m", N0),
    )
)

SPREAD = tuple(
    copy
    for b in (0, 64)
    for copy in ((N0, b, 64, "p", NM), (N0, b, 64, "m", N1), (NM, b, 32, "p", N2), (N1, b + 32, 32, "m", N2))
)

SETS = ((48, 32), (400, 208), (400, 208), (400, 208), (400, 208))
WEIGHTS = ((0, 0, "u"), (0, 0, "d"), (0, 0, "c"), (-2, 1, "u"), (-2, 0, "c"), (2, 2, "d"), (2, 0, "c"), (4, 1, "c"), (4, 2, "c"))


def where_am_i():
    t = lax.axis_index("tensor")
    return t, t // 4, lax.rem(t, 4)


def directions():
    _, xh, y = where_am_i()
    section = lax.axis_index("section")
    return {
        "p": {"tensor": xh * 4 + lax.rem(y + 1, 4)},
        "m": {"tensor": xh * 4 + lax.rem(y + 3, 4)},
        "x": {"tensor": (1 - xh) * 4 + y},
        "cross": {"dp": 1 - lax.axis_index("dp"), "tensor": (1 - xh) * 4 + y},
        "u": {"section": lax.rem(section + 2, 8)},
        "d": {"section": lax.rem(section + 6, 8)},
        "c": {"section": section + 1 - 2 * lax.rem(section, 2)},
    }


def slot_chunks():
    _, xh, y = where_am_i()
    near, far = xh * 4, (1 - xh) * 4
    up, down, opposite = lax.rem(y + 1, 4), lax.rem(y + 3, 4), lax.rem(y + 2, 4)
    return (near + y, far + y, near + up, near + down, far + up, far + down, near + opposite, far + opposite)


def remote(src, dst, send, recv, target):
    return pltpu.make_async_remote_copy(
        src_ref=src, dst_ref=dst, send_sem=send, recv_sem=recv, device_id=target, device_id_type=MESH
    )


def table_copies(table, buf, send, recv):
    where = directions()
    return [
        remote(buf.at[src, pl.ds(row, rows)], buf.at[dst, pl.ds(row, rows)], send.at[i], recv.at[i], where[way])
        for i, (src, row, rows, way, dst) in enumerate(table)
    ]


def weight_copies(number, source, buf, base, send, recv, source_base=0):
    rows, first = SETS[number]
    section = lax.axis_index("section")
    where = directions()

    def part(ref, offset, which, base=base):
        start = base + lax.rem(section + 8 + offset, 8) * rows
        start, count = ((start, rows), (start, first), (start + first, rows - first))[which]
        return ref.at[pl.ds(pl.multiple_of(start, 16), count)]

    copies = [remote(part(source, 0, 0, source_base), part(buf, 0, 0), send.at[number, 0], recv.at[number, 0], where["cross"])]
    for i, (offset, which, way) in enumerate(WEIGHTS):
        there = part(buf, offset, which)
        copies.append(remote(there, there, send.at[number, i + 1], recv.at[number, i + 1], where[way]))
    return copies


def merge_order(row0, rows):
    r = lax.broadcasted_iota(jnp.int32, (rows, CH), 0) + row0
    c = lax.broadcasted_iota(jnp.int32, (rows, CH), 1)
    a, b, i, j = r // 64, (r // 32) % 2, (r // 16) % 2, r % 16
    return ((2 * i + a) * 32 + 2 * j + b == c).astype(F32).astype(BF16)


def encode_kernel(
    patches, gain, w_hbm, q_gain, k_gain, layer_scale, wo_hbm, wp_hbm, counts, slots, feats,
    xg, w, qk, sums, q, k, v, wo, wp, mix, far, ob, proj, pieces, picked, arrive,
    w_sem, g_send, g_recv, s_send, s_recv, x_send, x_recv, m_send, m_recv, r_send, r_recv, e_send, e_recv,
    a_send, a_recv, b_send, b_recv,
):
    t, xh, y = where_am_i()
    opp = (1 - xh) * 4 + y
    chunk_of = slot_chunks()
    me = lax.axis_index("section") * 2 + lax.axis_index("dp")

    def group(index, tensor):
        return {"section": index // 2, "dp": lax.rem(index, 2), "tensor": tensor}

    w_copies = [pltpu.make_async_copy(w_hbm.at[j], w.at[j], w_sem.at[j]) for j in range(3)]
    own_copies = [
        pltpu.make_async_copy(wo_hbm, wo.at[pl.ds(0, LW)], w_sem.at[3]),
        pltpu.make_async_copy(wp_hbm, wp.at[0], w_sem.at[4]),
    ]
    for c in w_copies + own_copies:
        c.start()
    barrier = pltpu.get_barrier_semaphore()
    for n in range(1, 8):
        pl.semaphore_signal(barrier, inc=1, device_id={"tensor": lax.rem(t + n, 8)}, device_id_type=MESH)
    for way in ("cross", "u", "d", "c"):
        pl.semaphore_signal(barrier, inc=1, device_id=directions()[way], device_id_type=MESH)

    def norm(row0, rows):
        x = jnp.dot(merge_order(row0, rows), patches[...], preferred_element_type=F32)
        scale = lax.rsqrt(jnp.mean(x * x, axis=-1, keepdims=True) + EPS)
        xg[O0, pl.ds(row0, rows)] = (x * scale * gain[...].reshape(1, D)).astype(BF16)

    gc = table_copies(GATHER, xg, g_send, g_recv)
    wc = [weight_copies(0, wo_hbm, wo, LW, x_send, x_recv)]
    wc += [weight_copies(1 + ab, wp_hbm, wp.at[1], ab * D, x_send, x_recv, ab * D) for ab in range(4)]

    def weights_cross(n):
        wc[n][0].start()

    def weights_turn(n):
        wc[n][0].wait_recv()
        for i in (1, 2, 3):
            wc[n][i].start()

    def weights_forward(n):
        wc[n][1].wait_recv()
        wc[n][4].start()
        wc[n][5].start()
        wc[n][2].wait_recv()
        wc[n][6].start()
        wc[n][7].start()

    def weights_last(n):
        wc[n][4].wait_recv()
        wc[n][8].start()
        wc[n][6].wait_recv()
        wc[n][9].start()

    def weights_here(n):
        for i in (3, 5, 7, 8, 9):
            wc[n][i].wait_recv()

    norm(0, 32)
    norm(32, 32)
    norm(64, 32)
    pl.semaphore_wait(barrier, 11)
    weights_cross(0)
    for i in (0, 1, 2):
        gc[i].start()
    norm(96, 32)
    for i in (3, 4, 5):
        gc[i].start()
    for c in w_copies:
        c.wait()

    def after(done, *then):
        gc[done].wait_recv()
        for i in then:
            gc[i].start()

    def project_qk(g):
        x = xg[2 * g : 2 * g + 2].reshape(2 * CH, D)
        rows = pl.ds(2 * g * CH, 2 * CH)
        for j in range(2):
            part = jnp.dot(x, w[j], preferred_element_type=F32)
            qk[j, rows] = part
            for u in range(2):
                p = part[u * CH : (u + 1) * CH]
                sq = p * p
                sq = sq[:, :HD] + sq[:, HD : 2 * HD] + sq[:, 2 * HD :]
                row = jnp.sum(jnp.transpose(sq), axis=0, keepdims=True)
                sums[t, chunk_of[2 * g + u], :, j * HD : (j + 1) * HD] = row

    def project_v(g):
        x = xg[2 * g : 2 * g + 2].reshape(2 * CH, D)
        part = jnp.dot(x, w[2], preferred_element_type=F32).astype(BF16)
        for h in range(LH):
            v[h, pl.ds(2 * g * CH, 2 * CH), :HD] = part[:, h * HD : (h + 1) * HD]

    after(1, 6)
    after(2, 7)
    after(0, 8, 9)
    after(3, 12, 14)
    after(4, 13, 15)
    after(5)
    project_qk(0)
    project_v(0)
    weights_turn(0)
    after(8, 10)
    after(9, 11)
    after(12, 16)
    after(13, 17)
    weights_cross(1)
    project_qk(1)
    project_v(1)
    v[:, :, HD:] = jnp.ones((LH, 8 * CH, HD), BF16)
    weights_forward(0)
    after(14)
    after(15)
    project_qk(2)
    project_v(2)
    weights_last(0)
    for i in (6, 7, 16, 17, 10, 11):
        after(i)
    weights_cross(2)
    project_qk(3)

    s_copies = [
        remote(sums.at[t], sums.at[t], s_send.at[n], s_recv.at[n], {"tensor": lax.rem(t + n, 8)}) for n in range(1, 8)
    ]
    for c in gc:
        c.wait_send()
    for c in s_copies:
        c.start()
    project_v(3)
    weights_turn(1)
    for n in range(1, 8):
        there = sums.at[lax.rem(t + 8 - n, 8)]
        remote(there, there, s_send.at[n], s_recv.at[n], {"tensor": lax.rem(t + n, 8)}).wait_recv()
    def scale(slot, j):
        total = sums[0, chunk_of[slot], :, j * HD : (j + 1) * HD]
        for other in range(1, 8):
            total = total + sums[other, chunk_of[slot], :, j * HD : (j + 1) * HD]
        factor = lax.rsqrt(total / (HEADS * HD) + EPS)
        out, gains, extra = ((q, q_gain, HD**-0.5 * LOG2E), (k, k_gain, 1.0))[j]
        col = jnp.transpose(jnp.broadcast_to(factor, (CH, HD))) * extra
        gains = gains[...].reshape(1, LW)
        for h in range(LH):
            lanes = slice(h * HD, (h + 1) * HD)
            out[h, pl.ds(slot * CH, CH)] = (qk[j, pl.ds(slot * CH, CH), lanes] * col * gains[:, lanes]).astype(BF16)

    for slot in range(8):
        scale(slot, 1)

    def attend(slot, *places):
        scale(slot, 0)
        scale(slot + 1, 0)

        def one(h, _):
            rows = pl.ds(slot * CH, 2 * CH)
            scores = lax.dot_general(q[h, rows], k[h], (((1,), (1,)), ((), ())), preferred_element_type=F32)
            e = jnp.exp2(scores - jnp.max(scores, axis=-1, keepdims=True)).astype(BF16)
            part = jnp.dot(e, v[h], preferred_element_type=F32)
            part = (part[:, :HD] / part[:, HD:]).astype(BF16)
            lanes = pl.ds(pl.multiple_of(h * HD, HD), HD)
            for n, (dst, place) in enumerate(places):
                dst[place, :, lanes] = part[n * CH : (n + 1) * CH]
            return _

        lax.fori_loop(0, LH, one, 0)

    mc = [remote(far.at[n], mix.at[1, n], m_send.at[n], m_recv.at[n], directions()["x"]) for n in range(4)]
    rc = [
        remote(ob.at[src, pl.ds(row, 32)], xg.at[4 + i // 4, pl.ds(32 * (i % 4), 32)], r_send.at[i], r_recv.at[i], directions()[way])
        for i, (src, row, way, _) in enumerate(SCATTER)
    ]
    ec = table_copies(SPREAD, xg, e_send, e_recv)

    def branch(n, count):
        for i in range(n, n + count):
            mc[i].wait_recv()
        x = jnp.concatenate([mix[c, n : n + count].reshape(count * CH, LW) for c in range(2)], axis=1)
        for n0 in range(0, D, 1280):
            cols = slice(n0, min(n0 + 1280, D))
            part = jnp.dot(x, wo[:, cols], preferred_element_type=F32).astype(BF16)
            for i in range(count):
                ob[n + i, :, cols] = part[i * CH : (i + 1) * CH]

    def add(i):
        rc[i].wait_recv()
        _, row, _, dst = SCATTER[i]
        total = ob[dst, row : row + 32].astype(F32) + xg[4 + i // 4, 32 * (i % 4) : 32 * (i % 4) + 32].astype(F32)
        ob[dst, row : row + 32] = total.astype(BF16)

    own, off = mix.at[0], far
    attend(O2, (own, N2), (off, N2))
    mc[N2].start()
    attend(X1, (off, N1), (off, NM))
    mc[N1].start()
    mc[NM].start()
    own_copies[0].wait()
    weights_here(0)
    branch(N2, 1)
    for i in (0, 1, 6, 7):
        rc[i].start()
    attend(O1, (own, N1), (own, NM))
    branch(N1, 2)
    for i in (2, 4):
        rc[i].start()
    weights_turn(2)
    weights_cross(3)
    attend(O0, (own, N0), (off, N0))
    mc[N0].start()
    add(0)
    rc[3].start()
    add(1)
    rc[5].start()
    for i in (8, 10):
        rc[i].start()
    branch(N0, 1)
    weights_cross(4)
    add(6)
    rc[9].start()
    add(7)
    rc[11].start()
    weights_forward(1)
    weights_turn(3)

    def encode(row0):
        base = jnp.dot(merge_order(row0, 32), patches[...], preferred_element_type=F32)
        total = ob[N0, row0 : row0 + 32].astype(F32)
        xg[N0, pl.ds(row0, 32)] = (base + layer_scale[...].reshape(1, D) * total).astype(BF16)

    def encode_half(half):
        for i in (2, 4, 3, 5):
            add(6 * half + i)
        encode(64 * half)
        encode(64 * half + 32)
        ec[4 * half].start()
        ec[4 * half + 1].start()

    encode_half(0)
    weights_last(1)
    weights_forward(2)
    weights_turn(4)
    encode_half(1)
    weights_forward(3)
    weights_last(2)
    for c in rc + mc:
        c.wait_send()

    def forward(half):
        ec[4 * half].wait_recv()
        ec[4 * half + 2].start()
        ec[4 * half + 1].wait_recv()
        ec[4 * half + 3].start()

    def project(ab, c):
        x = xg[0:4, ab * 32 : (ab + 1) * 32, :].reshape(4 * 32, D)
        return jnp.dot(x, wp[c, ab * D : (ab + 1) * D, :], preferred_element_type=F32)

    forward(0)
    forward(1)
    weights_forward(4)
    weights_last(3)
    own_copies[1].wait()
    ec[2].wait_recv()
    ec[3].wait_recv()
    weights_here(1)
    weights_here(2)
    early = [project(0, c) + project(1, c) for c in range(2)]
    weights_last(4)
    ec[6].wait_recv()
    ec[7].wait_recv()
    weights_here(3)

    mine = me // 8 == xh

    def piece_copy(n, c):
        m = lax.rem(me + n, 8)
        target = group(8 * xh + m, (t, opp)[c])
        return remote(proj.at[c, m], pieces.at[me], a_send.at[c, n], a_recv.at[me], target)

    def first_copies(c, act):
        for n in range(1, 8):
            act(piece_copy(n, c))
        if c:
            act(piece_copy(0, 1))
        else:

            @pl.when(jnp.logical_not(mine))
            def _():
                act(piece_copy(0, 0))

    for c in range(2):
        out = early[c] + project(2, c)
        if c == 0:
            weights_here(4)
        out = (out + project(3, c)).astype(BF16)
        for n, slot in ((N2, O2), (N1, O1), (NM, OM), (N0, O0)):
            place = 2 * lax.rem(chunk_of[slot], 4)
            proj[c, pl.ds(place, 2)] = out[n * 32 : (n + 1) * 32].reshape(2, 16, 512)
        first_copies(c, lambda copy: copy.start())

    @pl.when(mine)
    def _():
        pieces[me] = proj[0, lax.rem(me, 8)]

    def piece_here(g):
        remote(pieces.at[g], pieces.at[g], a_send.at[0, 0], a_recv.at[g], group(me, opp)).wait_recv()

    for n in range(1, 16):
        piece_here(lax.rem(me + n, 16))

    @pl.when(jnp.logical_not(mine))
    def _():
        piece_here(me)

    start = jnp.int32(0)
    for g in range(16):
        for s in range(2):
            tile = slots[jnp.minimum(start + s, 15)]
            picked[g, s] = pieces[tile]
        start = start + counts[g]
    second = [
        remote(
            picked.at[lax.rem(me + n, 16)], arrive.at[me], b_send.at[n], b_recv.at[n], group(lax.rem(me + n, 16), t)
        )
        for n in range(1, 16)
    ]
    for c in second:
        c.start()
    arrive[me] = picked[me]
    for n in range(1, 16):
        there = arrive.at[lax.rem(me + 16 - n, 16)]
        remote(there, there, b_send.at[n], b_recv.at[n], group(lax.rem(me + n, 16), t)).wait_recv()
    for n in range(16):
        for s in range(2):
            feats[s * 256 + n * 16 : s * 256 + n * 16 + 16, :] = arrive[n, s]
    for c in range(2):
        first_copies(c, lambda copy: copy.wait_send())
    for c in s_copies + second + ec + [c for copies in wc for c in copies]:
        c.wait_send()


def place_kernel(feats, text_hbm, counts, offsets, out, text, sem):
    copy = pltpu.make_async_copy(text_hbm, text, sem)
    copy.start()
    me = lax.axis_index("section") * 2 + lax.axis_index("dp")
    rows = counts[me] * 256
    offset = offsets[me]
    seq = text.shape[0]
    r = lax.broadcasted_iota(jnp.int32, (seq, 512), 0) - offset
    c = lax.broadcasted_iota(jnp.int32, (seq, 512), 1)
    pick = (r == c).astype(F32).astype(BF16)
    moved = jnp.dot(pick, feats[...], preferred_element_type=F32).astype(BF16)
    copy.wait()
    out[...] = jnp.where((r >= 0) & (r < rows), moved, text[...])


def spec(space):
    return pl.BlockSpec(memory_space=space)


def shards(
    patches,
    norm_gain,
    w_qkv,
    q_gain,
    k_gain,
    w_out,
    layer_scale,
    w_proj,
    text_embed,
    tile_counts,
    image_offsets,
    tile_slots,
):
    dma = pltpu.SemaphoreType.DMA
    smem = pltpu.SMEM
    heads = VMEM((LH, 8 * CH, HD), BF16)
    values = VMEM((LH, 8 * CH, 2 * HD), BF16)
    feats = pl.pallas_call(
        encode_kernel,
        out_shape=jax.ShapeDtypeStruct((512, 512), BF16),
        in_specs=[spec(s) for s in (VMEM, VMEM, pl.ANY, VMEM, VMEM, VMEM, pl.ANY, pl.ANY, smem, smem)],
        out_specs=spec(VMEM),
        scratch_shapes=[
            VMEM((8, CH, D), BF16),
            VMEM((3, D, LW), BF16),
            VMEM((2, 8 * CH, LW), F32),
            VMEM((8, 8, 1, 2 * HD), F32),
            heads,
            heads,
            values,
            VMEM((2 * LW, D), BF16),
            VMEM((2, 4 * D, 512), BF16),
            VMEM((2, 4, CH, LW), BF16),
            VMEM((4, CH, LW), BF16),
            VMEM((4, CH, D), BF16),
            VMEM((2, 8, 16, 512), BF16),
            VMEM((16, 16, 512), BF16),
            VMEM((16, 2, 16, 512), BF16),
            VMEM((16, 2, 16, 512), BF16),
            dma((5,)),
            dma((len(GATHER),)),
            dma((len(GATHER),)),
            dma((8,)),
            dma((8,)),
            dma((len(SETS), 10)),
            dma((len(SETS), 10)),
            dma((4,)),
            dma((4,)),
            dma((len(SCATTER),)),
            dma((len(SCATTER),)),
            dma((len(SPREAD),)),
            dma((len(SPREAD),)),
            dma((2, 8)),
            dma((16,)),
            dma((16,)),
            dma((16,)),
        ],
        compiler_params=pltpu.CompilerParams(collective_id=0, **PARAMS),
        name="encode",
    )(
        patches[0],
        norm_gain,
        w_qkv.transpose(1, 0, 2),
        q_gain,
        k_gain,
        layer_scale,
        w_out,
        w_proj,
        tile_counts,
        tile_slots,
    )
    out = pl.pallas_call(
        place_kernel,
        out_shape=jax.ShapeDtypeStruct(text_embed.shape[1:], BF16),
        in_specs=[spec(s) for s in (VMEM, pl.ANY, smem, smem)],
        out_specs=spec(VMEM),
        scratch_shapes=[VMEM(text_embed.shape[1:], BF16), pltpu.SemaphoreType.DMA],
        compiler_params=pltpu.CompilerParams(vmem_limit_bytes=62 * 1024 * 1024),
        name="place",
    )(feats, text_embed[0], tile_counts, image_offsets)
    return out[None]


def solution(mesh):
    placed = (
        P(("section", "dp"), "tensor", None),
        P(),
        P(None, None, "tensor"),
        P("tensor"),
        P("tensor"),
        P("tensor", None),
        P(),
        P(None, "tensor"),
        P(("section", "dp"), None, "tensor"),
        P(),
        P(),
        P(),
    )
    return jax.shard_map(
        shards,
        mesh=mesh,
        in_specs=placed,
        out_specs=P(("section", "dp"), None, "tensor"),
        check_vma=False,
    )
```
